32 devices in a mesh: lat: 4 (over y, core), lon: 8 (over z, x).
Axes of the slice: x: 2, y: 2, z: 4, core: 2. Of those that a mesh axis runs over, the one named last changes fastest.
Arguments:
- residual: bfloat16 [128, 128, 128], P('lat', 'lon'), may hold values from -6 to 6
- noise_weights: float32 [128, 128], P('lat', 'lon'), may hold values from 0.5 to 4
- kernel: bfloat16 [4, 1, 2048, 2048], P(None, None, 'lat'), may hold values from -0.0625 to 0.0625
Outputs:
- gradient: float32 [1, 128, 128, 128], P(None, 'lat', 'lon')
The draws below stay inside these ranges and needn't reach their ends.
All inputs are finite; a program needn't handle non-finite values.
Results may differ from the reference program's by a relative error of at most 0.0029.
Values may be sent and summed in bfloat16 or wider, within the bound.
A program may use at most 64 MiB of HBM per device.

```python
import math
import jax
import jax.numpy as jnp

LON_DEV = 16
PROBES = 128
LAYERS = 1
OFFSETS = 4
NY = 128
NX = 128
CELLS = 2048
N_LON = 8


def block_levels(stream_key, shape, split, least, top_value):
    loudness = 1.0
    for position, blocks in split:
        heights = jax.random.uniform(jax.random.fold_in(jax.random.fold_in(stream_key, 6), position), (blocks,), jnp.float32, least / len(split), top_value / len(split))
        loudness = loudness * jnp.repeat(jnp.exp(heights), shape[position] // blocks).reshape((-1,) + (1,) * (len(shape) - 1 - position))
    return loudness


def gaussian(stream_key, dims, scale, reach, cuts=(), kind=jnp.bfloat16):
    entries = jax.random.normal(stream_key, dims, jnp.float32) * scale
    if len(cuts) > 0:
        entries = block_levels(stream_key, dims, cuts, -0.22, 0.18) * entries
    return jnp.clip(entries, min=-reach, max=reach).astype(kind)


def setup_inputs(seed: int = 0) -> dict:
    key_list = jax.random.split(jax.random.key(seed), 4)
    residual = gaussian(key_list[0], (NY, NX, PROBES), 1.0, 6.0, ((0, 4), (1, 8)))
    noise_weights = jnp.clip(jnp.exp(math.log(4.0) - 2.0794415 * jax.random.uniform(key_list[1], (NY, NX), jnp.float32) ** block_levels(key_list[1], (NY, NX), ((0, 4), (1, 8)), -0.2, 0.2)), 0.5, 4.0)
    kernel = gaussian(key_list[2], (OFFSETS, LAYERS, CELLS, CELLS), (OFFSETS * CELLS) ** -0.5, 0.0625, ((2, 4),))
    return {"residual": residual, "noise_weights": noise_weights, "kernel": kernel}


def reference(residual, noise_weights, kernel):
    weighted = (noise_weights[:, :, None] * residual.astype(jnp.float32)).astype(jnp.bfloat16)
    blocks = weighted.reshape(NY, N_LON, LON_DEV, PROBES).transpose(1, 0, 2, 3)
    blocks = blocks.reshape(N_LON, NY * LON_DEV, PROBES).astype(jnp.float32)
    summed = jnp.zeros((N_LON, LAYERS, NY * LON_DEV, PROBES), jnp.float32)
    for offset in range(OFFSETS):
        shifted = jnp.roll(blocks, offset, axis=0)
        summed = summed + jnp.einsum("lqc,jqp->jlcp", kernel[offset].astype(jnp.float32), shifted)
    summed = summed.reshape(N_LON, LAYERS, NY, LON_DEV, PROBES).transpose(1, 2, 0, 3, 4)
    return summed.reshape(LAYERS, NY, NX, PROBES)
```

```python
import functools

import jax
import jax.numpy as jnp
from jax import lax
from jax.experimental import pallas as pl
from jax.experimental.pallas import tpu as pltpu
from jax.sharding import PartitionSpec as P

MESH = pl.DeviceIdType.MESH


def sweep(
    lats, lons, res_ref, nw_ref, panel_hbm, out_ref,
    panel, blocks, total, outgoing, incoming,
    panel_sem, east_send, east_recv, band_send, band_recv,
):
    offsets, layers, rows, cells = panel_hbm.shape
    probes = res_ref.shape[-1]
    band = cells // lats
    lat, lon = lax.axis_index("lat"), lax.axis_index("lon")

    loads = []
    for d in range(offsets):
        for l in range(layers):
            load = pltpu.make_async_copy(
                panel_hbm.at[d, l], panel.at[d, l], panel_sem.at[d, l]
            )
            load.start()
            loads.append(load)

    barrier = pltpu.get_barrier_semaphore()
    for d in range(1, offsets):
        pl.semaphore_signal(
            barrier, inc=1, device_id=(lat, lax.rem(lon + lons - d, lons)), device_id_type=MESH
        )
    for s in range(1, lats):
        pl.semaphore_signal(
            barrier, inc=1, device_id=(lax.rem(lat + s, lats), lon), device_id_type=MESH
        )

    weighted = nw_ref[...][:, :, None] * res_ref[...].astype(jnp.float32)
    blocks[0] = weighted.reshape(rows, probes).T.astype(jnp.bfloat16)

    pl.semaphore_wait(barrier, offsets - 1 + lats - 1)
    east = []
    for d in range(1, offsets):
        copy = pltpu.make_async_remote_copy(
            src_ref=blocks.at[0],
            dst_ref=blocks.at[d],
            send_sem=east_send.at[d - 1],
            recv_sem=east_recv.at[d - 1],
            device_id=(lat, lax.rem(lon + d, lons)),
            device_id_type=MESH,
        )
        copy.start()
        east.append(copy)

    def term(d, l, first):
        columns = pl.ds(pl.multiple_of(first, band), band)
        return columns, jnp.dot(
            blocks[d], panel[d, l, :, columns], preferred_element_type=jnp.float32
        )

    for d in range(offsets - 1):
        for l in range(layers):
            loads[d * layers + l].wait()
        if d > 0:
            east[d - 1].wait_recv()
        for l in range(layers):
            for b in range(lats):
                columns, value = term(d, l, b * band)
                if d == 0:
                    total[l, :, columns] = value
                else:
                    total[l, :, columns] += value

    last = offsets - 1
    for l in range(layers):
        loads[last * layers + l].wait()
    east[last - 1].wait_recv()
    sent = []
    for s in range(1, lats):
        to = lax.rem(lat + s, lats)
        for l in range(layers):
            columns, value = term(last, l, to * band)
            outgoing[s - 1, l] = (total[l, :, columns] + value).astype(jnp.bfloat16)
        copy = pltpu.make_async_remote_copy(
            src_ref=outgoing.at[s - 1],
            dst_ref=incoming.at[s - 1],
            send_sem=band_send.at[s - 1],
            recv_sem=band_recv.at[s - 1],
            device_id=(to, lon),
            device_id_type=MESH,
        )
        copy.start()
        sent.append(copy)
    own = []
    for l in range(layers):
        columns, value = term(last, l, lat * band)
        own.append(total[l, :, columns] + value)
    for copy in sent:
        copy.wait_recv()
    for l in range(layers):
        value = own[l]
        for s in range(1, lats):
            value = value + incoming[s - 1, l].astype(jnp.float32)
        out_ref[l] = value.T.reshape(out_ref.shape[1:])
    for copy in east + sent:
        copy.wait_send()


def per_device(lats, lons, residual, noise_weights, kernel):
    offsets, layers, rows, cells = kernel.shape
    probes = residual.shape[2]
    band = cells // lats
    vmem = pl.BlockSpec(memory_space=pltpu.VMEM)
    return pl.pallas_call(
        functools.partial(sweep, lats, lons),
        out_shape=jax.ShapeDtypeStruct(
            (layers, residual.shape[0], residual.shape[1], probes), jnp.float32
        ),
        in_specs=[vmem, vmem, pl.BlockSpec(memory_space=pl.ANY)],
        out_specs=vmem,
        scratch_shapes=[
            pltpu.VMEM((offsets, layers, rows, cells), jnp.bfloat16),
            pltpu.VMEM((offsets, probes, rows), jnp.bfloat16),
            pltpu.VMEM((layers, probes, cells), jnp.float32),
            pltpu.VMEM((lats - 1, layers, probes, band), jnp.bfloat16),
            pltpu.VMEM((lats - 1, layers, probes, band), jnp.bfloat16),
            pltpu.SemaphoreType.DMA((offsets, layers)),
            pltpu.SemaphoreType.DMA((offsets - 1,)),
            pltpu.SemaphoreType.DMA((offsets - 1,)),
            pltpu.SemaphoreType.DMA((lats - 1,)),
            pltpu.SemaphoreType.DMA((lats - 1,)),
        ],
        compiler_params=pltpu.CompilerParams(
            collective_id=0, has_side_effects=True, vmem_limit_bytes=48 * 1024 * 1024
        ),
        cost_estimate=pl.CostEstimate(
            flops=2 * offsets * layers * rows * cells * probes,
            bytes_accessed=2 * offsets * layers * rows * cells,
            transcendentals=0,
        ),
    )(residual, noise_weights, kernel)


def solution(mesh):
    return jax.shard_map(
        functools.partial(per_device, mesh.shape["lat"], mesh.shape["lon"]),
        mesh=mesh,
        in_specs=(P("lat", "lon", None), P("lat", "lon"), P(None, None, "lat", None)),
        out_specs=P(None, "lat", "lon", None),
        check_vma=False,
    )
```

```python
import functools

import jax
import jax.numpy as jnp
from jax import lax
from jax.experimental import pallas as pl
from jax.experimental.pallas import tpu as pltpu
from jax.sharding import PartitionSpec as P

MESH = pl.DeviceIdType.MESH


def route(offsets, lons):
    if lons % 2 or offsets < 3:
        table = {d: (-d, 0) for d in range(1, offsets)}
        return 1, [table], list(range(1, offsets))
    even, odd = {}, {}
    for d in range(1, offsets):
        even[d] = (1, 2) if d == 1 else (-2, d - 2)
        odd[d] = (-1, d - 1) if d % 2 else (-2, d - 2)
    return 2, [even, odd], list(range(2, offsets, 2)) + list(range(1, offsets, 2))


def sweep(
    lats, lons, res_hbm, nw_hbm, panel_hbm, out_ref,
    res, nw, panel, blocks, total, outgoing, incoming, summed,
    input_sem, panel_sem, east_send, east_recv, band_send, band_recv,
):
    offsets, layers, rows, cells = panel_hbm.shape
    probes = res_hbm.shape[-1]
    chunks, part = outgoing.shape[0], outgoing.shape[3]
    band = cells // lats
    lat, lon = lax.axis_index("lat"), lax.axis_index("lon")
    period, source, order = route(offsets, lons)
    pair = 2 if lats % 2 == 0 else 1
    groups = lats // pair

    res_load = pltpu.make_async_copy(res_hbm, res, input_sem.at[0])
    nw_load = pltpu.make_async_copy(nw_hbm, nw, input_sem.at[1])
    res_load.start()
    nw_load.start()
    loads = {}
    for d in [0] + order:
        loads[d] = pltpu.make_async_copy(panel_hbm.at[d], panel.at[d], panel_sem.at[d])
        loads[d].start()

    def along(delta):
        return (lat, lax.rem(lon + (delta + lons), lons))

    def across(a, b):
        to = lax.rem(lat // pair + a, groups) * pair + lax.rem(lat % pair + b, pair)
        return (to, lon)

    partners = [(a, b) for a in range(groups - 1, -1, -1) for b in range(pair)][: lats]
    partners = [ab for ab in partners if ab != (0, 0)]

    sends = [[] for _ in range(period)]
    senders = [set() for _ in range(period)]
    for q in range(period):
        for d in order:
            delta, held = source[q][d]
            sends[(q + delta) % period].append((-delta, held, d))
            senders[q].add(delta)

    def per_parity(action):
        for q in range(period):
            if period == 1:
                action(q)
            else:
                pl.when(lax.rem(lon, period) == q)(functools.partial(action, q))

    barrier = pltpu.get_barrier_semaphore()

    def greet(q):
        for delta in sorted(senders[q]):
            pl.semaphore_signal(barrier, inc=1, device_id=along(delta), device_id_type=MESH)

    per_parity(greet)
    for a, b in partners:
        pl.semaphore_signal(barrier, inc=1, device_id=across(a, b), device_id_type=MESH)

    res_load.wait()
    nw_load.wait()
    columns = res.shape[1]
    pieces = [
        nw[:, y : y + 1] * res[y].astype(jnp.float32) for y in range(rows // columns)
    ]
    blocks[0] = jnp.concatenate(pieces, axis=0).T.astype(jnp.bfloat16)

    def chunk(c):
        return pl.ds(c * part, part)

    def east(q, n, c):
        delta, held, d = sends[q][n]
        return pltpu.make_async_remote_copy(
            src_ref=blocks.at[held, chunk(c)],
            dst_ref=blocks.at[d, chunk(c)],
            send_sem=east_send.at[n, c],
            recv_sem=east_recv.at[d, c],
            device_id=along(delta),
            device_id_type=MESH,
        )

    def forward(held, cs):
        def action(q):
            for c in cs:
                for n, send in enumerate(sends[q]):
                    if send[1] == held:
                        east(q, n, c).start()

        per_parity(action)

    def arrive(d, c):
        pltpu.make_async_remote_copy(
            src_ref=blocks.at[d, chunk(c)],
            dst_ref=blocks.at[d, chunk(c)],
            send_sem=east_send.at[0, c],
            recv_sem=east_recv.at[d, c],
            device_id=along(1),
            device_id_type=MESH,
        ).wait_recv()

    pl.semaphore_wait(barrier, len(senders[0]) + len(partners))
    forward(0, range(chunks))

    def accumulate(d, first):
        loads[d].wait()
        for l in range(layers):

            @pl.loop(0, lats)
            def _(b):
                cols = pl.ds(pl.multiple_of(b * band, band), band)
                value = jnp.dot(
                    blocks[d], panel[d, l, :, cols], preferred_element_type=jnp.float32
                )
                total[l, :, cols] = value if first else total[l, :, cols] + value

    accumulate(0, True)
    for d in order[:-1]:
        for c in range(chunks):
            arrive(d, c)
            forward(d, [c])
        accumulate(d, False)

    last = order[-1]
    loads[last].wait()

    def finish(c, to):
        cols = pl.ds(pl.multiple_of(to * band, band), band)
        return [
            total[l, chunk(c), cols]
            + jnp.dot(
                blocks[last, chunk(c)], panel[last, l, :, cols],
                preferred_element_type=jnp.float32,
            )
            for l in range(layers)
        ]

    sent = {}
    for c in range(chunks):
        arrive(last, c)
        for n, (a, b) in enumerate(partners):
            to = across(a, b)
            for l, value in enumerate(finish(c, to[0])):
                outgoing[c, n, l] = value.astype(jnp.bfloat16)
            sent[c, n] = pltpu.make_async_remote_copy(
                src_ref=outgoing.at[c, n],
                dst_ref=incoming.at[c, n],
                send_sem=band_send.at[c, n],
                recv_sem=band_recv.at[c, n],
                device_id=to,
                device_id_type=MESH,
            )
            sent[c, n].start()
        for l, value in enumerate(finish(c, lat)):
            summed[l, chunk(c)] = value
    for c in range(chunks):
        for n in reversed(range(len(partners))):
            sent[c, n].wait_recv()
        for l in range(layers):
            value = summed[l, chunk(c)]
            for n in range(len(partners)):
                value = value + incoming[c, n, l].astype(jnp.float32)
            summed[l, chunk(c)] = value
    for l in range(layers):
        out_ref[l] = summed[l].T.reshape(out_ref.shape[1:])

    def drain(q):
        for c in range(chunks):
            for n in range(len(sends[q])):
                east(q, n, c).wait_send()

    per_parity(drain)
    for copy in sent.values():
        copy.wait_send()


def per_device(lats, lons, residual, noise_weights, kernel):
    offsets, layers, rows, cells = kernel.shape
    probes = residual.shape[2]
    band = cells // lats
    chunks = 2 if probes % 32 == 0 else 1
    part = probes // chunks
    remote = pl.BlockSpec(memory_space=pltpu.HBM)
    return pl.pallas_call(
        functools.partial(sweep, lats, lons),
        out_shape=jax.ShapeDtypeStruct(
            (layers, residual.shape[0], residual.shape[1], probes), jnp.float32
        ),
        in_specs=[remote, remote, remote],
        out_specs=pl.BlockSpec(memory_space=pltpu.VMEM),
        scratch_shapes=[
            pltpu.VMEM(residual.shape, jnp.bfloat16),
            pltpu.VMEM(noise_weights.shape[::-1], jnp.float32),
            pltpu.VMEM((offsets, layers, rows, cells), jnp.bfloat16),
            pltpu.VMEM((offsets, probes, rows), jnp.bfloat16),
            pltpu.VMEM((layers, probes, cells), jnp.float32),
            pltpu.VMEM((chunks, lats - 1, layers, part, band), jnp.bfloat16),
            pltpu.VMEM((chunks, lats - 1, layers, part, band), jnp.bfloat16),
            pltpu.VMEM((layers, probes, band), jnp.float32),
            pltpu.SemaphoreType.DMA((2,)),
            pltpu.SemaphoreType.DMA((offsets,)),
            pltpu.SemaphoreType.DMA((2 * offsets, chunks)),
            pltpu.SemaphoreType.DMA((offsets, chunks)),
            pltpu.SemaphoreType.DMA((chunks, lats - 1)),
            pltpu.SemaphoreType.DMA((chunks, lats - 1)),
        ],
        compiler_params=pltpu.CompilerParams(
            collective_id=0, has_side_effects=True, vmem_limit_bytes=63 * 1024 * 1024
        ),
        cost_estimate=pl.CostEstimate(
            flops=2 * offsets * layers * rows * cells * probes,
            bytes_accessed=2 * offsets * layers * rows * cells,
            transcendentals=0,
        ),
    )(residual, noise_weights.T, kernel)


def solution(mesh):
    return jax.shard_map(
        functools.partial(per_device, mesh.shape["lat"], mesh.shape["lon"]),
        mesh=mesh,
        in_specs=(P("lat", "lon", None), P("lat", "lon"), P(None, None, "lat", None)),
        out_specs=P(None, "lat", "lon", None),
        check_vma=False,
    )
```

```python
import functools

import jax
import jax.numpy as jnp
from jax import lax
from jax.experimental import pallas as pl
from jax.experimental.pallas import tpu as pltpu
from jax.sharding import PartitionSpec as P

MESH = pl.DeviceIdType.MESH


def route(offsets, lons):
    if lons % 2 or offsets < 3:
        table = {d: (-d, 0) for d in range(1, offsets)}
        return 1, [table], list(range(1, offsets))
    even, odd = {}, {}
    for d in range(1, offsets):
        even[d] = (1, 2) if d == 1 else (-2, d - 2)
        odd[d] = (-1, d - 1) if d % 2 else (-2, d - 2)
    return 2, [even, odd], list(range(2, offsets, 2)) + list(range(1, offsets, 2))


def sweep(
    lats, lons, res_hbm, nw_hbm, panel_hbm, out_ref,
    res, nw, panel, blocks, total, chip_out, chip_in, band_out, band_in, summed,
    input_sem, panel_sem, east_send, east_recv, chip_send, chip_recv, band_send, band_recv,
):
    offsets, layers, rows, cells = panel_hbm.shape
    probes = res_hbm.shape[-1]
    chunks, part = band_out.shape[0], band_out.shape[3]
    band = cells // lats
    lat, lon = lax.axis_index("lat"), lax.axis_index("lon")
    period, source, order = route(offsets, lons)
    pair = 2 if lats % 2 == 0 else 1
    groups = lats // pair

    res_load = pltpu.make_async_copy(res_hbm, res, input_sem.at[0])
    nw_load = pltpu.make_async_copy(nw_hbm, nw, input_sem.at[1])
    res_load.start()
    nw_load.start()
    loads = {}
    for d in [0] + order:
        loads[d] = pltpu.make_async_copy(panel_hbm.at[d], panel.at[d], panel_sem.at[d])
        loads[d].start()

    def along(delta):
        return (lat, lax.rem(lon + (delta + lons), lons))

    def across(a, b):
        to = lax.rem(lat // pair + a, groups) * pair + lax.rem(lat % pair + b, pair)
        return (to, lon)

    partners = [(a, 0) for a in range(1, groups)] + [(0, b) for b in range(1, pair)]

    sends = [[] for _ in range(period)]
    senders = [set() for _ in range(period)]
    for q in range(period):
        for d in order:
            delta, held = source[q][d]
            sends[(q + delta) % period].append((-delta, held, d))
            senders[q].add(delta)

    def per_parity(action):
        for q in range(period):
            if period == 1:
                action(q)
            else:
                pl.when(lax.rem(lon, period) == q)(functools.partial(action, q))

    barrier = pltpu.get_barrier_semaphore()

    def greet(q):
        for delta in sorted(senders[q]):
            pl.semaphore_signal(barrier, inc=1, device_id=along(delta), device_id_type=MESH)

    per_parity(greet)
    for a, b in partners:
        pl.semaphore_signal(barrier, inc=1, device_id=across(a, b), device_id_type=MESH)

    res_load.wait()
    nw_load.wait()
    columns = res.shape[1]
    pieces = [
        nw[:, y : y + 1] * res[y].astype(jnp.float32) for y in range(rows // columns)
    ]
    blocks[0] = jnp.concatenate(pieces, axis=0).T.astype(jnp.bfloat16)

    def chunk(c):
        return pl.ds(c * part, part)

    def east(q, n, c):
        delta, held, d = sends[q][n]
        return pltpu.make_async_remote_copy(
            src_ref=blocks.at[held, chunk(c)],
            dst_ref=blocks.at[d, chunk(c)],
            send_sem=east_send.at[n, c],
            recv_sem=east_recv.at[d, c],
            device_id=along(delta),
            device_id_type=MESH,
        )

    def forward(held, cs):
        def action(q):
            for c in cs:
                for n, send in enumerate(sends[q]):
                    if send[1] == held:
                        east(q, n, c).start()

        per_parity(action)

    def arrive(d, c):
        pltpu.make_async_remote_copy(
            src_ref=blocks.at[d, chunk(c)],
            dst_ref=blocks.at[d, chunk(c)],
            send_sem=east_send.at[0, c],
            recv_sem=east_recv.at[d, c],
            device_id=along(1),
            device_id_type=MESH,
        ).wait_recv()

    pl.semaphore_wait(barrier, len(senders[0]) + len(partners))
    forward(0, [0])

    def follow(q):
        for c in range(1, chunks):
            for n, send in enumerate(sends[q]):
                if send[1] == 0:
                    east(q, n, c - 1).wait_send()
                    east(q, n, c).start()

    per_parity(follow)

    def accumulate(d, first):
        loads[d].wait()
        for l in range(layers):

            @pl.loop(0, lats)
            def _(b):
                cols = pl.ds(pl.multiple_of(b * band, band), band)
                value = jnp.dot(
                    blocks[d], panel[d, l, :, cols], preferred_element_type=jnp.float32
                )
                total[l, :, cols] = value if first else total[l, :, cols] + value

    accumulate(0, True)
    for d in order[:-1]:
        for c in range(chunks):
            arrive(d, c)
            forward(d, [c])
        accumulate(d, False)

    last = order[-1]
    loads[last].wait()

    def finish(c, to):
        cols = pl.ds(pl.multiple_of(to * band, band), band)
        return [
            total[l, chunk(c), cols]
            + jnp.dot(
                blocks[last, chunk(c)], panel[last, l, :, cols],
                preferred_element_type=jnp.float32,
            )
            for l in range(layers)
        ]

    def inner(c, b):
        return pltpu.make_async_remote_copy(
            src_ref=chip_out.at[c, b - 1],
            dst_ref=chip_in.at[c, b - 1],
            send_sem=chip_send.at[c, b - 1],
            recv_sem=chip_recv.at[c, b - 1],
            device_id=across(0, b),
            device_id_type=MESH,
        )

    def outer(c, a):
        return pltpu.make_async_remote_copy(
            src_ref=band_out.at[c, a - 1],
            dst_ref=band_in.at[c, a - 1],
            send_sem=band_send.at[c, a - 1],
            recv_sem=band_recv.at[c, a - 1],
            device_id=across(a, 0),
            device_id_type=MESH,
        )

    for c in range(chunks):
        arrive(last, c)
        for b in range(1, pair):
            for a in range(groups):
                for l, value in enumerate(finish(c, across(a, b)[0])):
                    chip_out[c, b - 1, a, l] = value.astype(jnp.bfloat16)
            inner(c, b).start()
        mine = [finish(c, across(a, 0)[0]) for a in range(groups)]
        for b in range(1, pair):
            inner(c, b).wait_recv()
        for a in list(range(1, groups)) + [0]:
            for l in range(layers):
                value = mine[a][l]
                for b in range(1, pair):
                    value = value + chip_in[c, b - 1, a, l].astype(jnp.float32)
                if a == 0:
                    summed[l, chunk(c)] = value
                else:
                    band_out[c, a - 1, l] = value.astype(jnp.bfloat16)
            if a > 0:
                outer(c, a).start()
    for c in range(chunks):
        for a in range(1, groups):
            outer(c, a).wait_recv()
        for l in range(layers):
            value = summed[l, chunk(c)]
            for a in range(1, groups):
                value = value + band_in[c, a - 1, l].astype(jnp.float32)
            summed[l, chunk(c)] = value
    for l in range(layers):
        out_ref[l] = summed[l].T.reshape(out_ref.shape[1:])

    def drain(q):
        for c in range(chunks):
            for n, send in enumerate(sends[q]):
                if send[1] > 0 or c == chunks - 1:
                    east(q, n, c).wait_send()

    per_parity(drain)
    for c in range(chunks):
        for b in range(1, pair):
            inner(c, b).wait_send()
        for a in range(1, groups):
            outer(c, a).wait_send()


def per_device(lats, lons, residual, noise_weights, kernel):
    offsets, layers, rows, cells = kernel.shape
    probes = residual.shape[2]
    band = cells // lats
    chunks = 2 if probes % 32 == 0 else 1
    part = probes // chunks
    pair = 2 if lats % 2 == 0 else 1
    groups = lats // pair
    inner, outer = max(pair - 1, 1), max(groups - 1, 1)
    remote = pl.BlockSpec(memory_space=pltpu.HBM)
    return pl.pallas_call(
        functools.partial(sweep, lats, lons),
        out_shape=jax.ShapeDtypeStruct(
            (layers, residual.shape[0], residual.shape[1], probes), jnp.float32
        ),
        in_specs=[remote, remote, remote],
        out_specs=pl.BlockSpec(memory_space=pltpu.VMEM),
        scratch_shapes=[
            pltpu.VMEM(residual.shape, jnp.bfloat16),
            pltpu.VMEM(noise_weights.shape[::-1], jnp.float32),
            pltpu.VMEM((offsets, layers, rows, cells), jnp.bfloat16),
            pltpu.VMEM((offsets, probes, rows), jnp.bfloat16),
            pltpu.VMEM((layers, probes, cells), jnp.float32),
            pltpu.VMEM((chunks, inner, groups, layers, part, band), jnp.bfloat16),
            pltpu.VMEM((chunks, inner, groups, layers, part, band), jnp.bfloat16),
            pltpu.VMEM((chunks, outer, layers, part, band), jnp.bfloat16),
            pltpu.VMEM((chunks, outer, layers, part, band), jnp.bfloat16),
            pltpu.VMEM((layers, probes, band), jnp.float32),
            pltpu.SemaphoreType.DMA((2,)),
            pltpu.SemaphoreType.DMA((offsets,)),
            pltpu.SemaphoreType.DMA((2 * offsets, chunks)),
            pltpu.SemaphoreType.DMA((offsets, chunks)),
            pltpu.SemaphoreType.DMA((chunks, inner)),
            pltpu.SemaphoreType.DMA((chunks, inner)),
            pltpu.SemaphoreType.DMA((chunks, outer)),
            pltpu.SemaphoreType.DMA((chunks, outer)),
        ],
        compiler_params=pltpu.CompilerParams(
            collective_id=0, has_side_effects=True, vmem_limit_bytes=63 * 1024 * 1024
        ),
        cost_estimate=pl.CostEstimate(
            flops=2 * offsets * layers * rows * cells * probes,
            bytes_accessed=2 * offsets * layers * rows * cells,
            transcendentals=0,
        ),
    )(residual, noise_weights.T, kernel)


def solution(mesh):
    return jax.shard_map(
        functools.partial(per_device, mesh.shape["lat"], mesh.shape["lon"]),
        mesh=mesh,
        in_specs=(P("lat", "lon", None), P("lat", "lon"), P(None, None, "lat", None)),
        out_specs=P(None, "lat", "lon", None),
        check_vma=False,
    )
```

```python
import functools

import jax
import jax.numpy as jnp
from jax import lax
from jax.experimental import pallas as pl
from jax.experimental.pallas import tpu as pltpu
from jax.sharding import PartitionSpec as P

MESH = pl.DeviceIdType.MESH


def route(offsets, lons):
    if lons % 2 or offsets < 3:
        table = {d: (-d, 0) for d in range(1, offsets)}
        return 1, [table], list(range(1, offsets))
    even, odd = {}, {}
    for d in range(1, offsets):
        even[d] = (1, 2) if d == 1 else (-2, d - 2)
        odd[d] = (-1, d - 1) if d % 2 else (-2, d - 2)
    return 2, [even, odd], list(range(2, offsets, 2)) + list(range(1, offsets, 2))


def sweep(
    lats, lons, res_hbm, nw_hbm, panel_hbm, out_ref,
    res, nw, panel, blocks, total, chip_out, chip_in, band_out, band_in,
    input_sem, panel_sem, east_send, east_recv, chip_send, chip_recv, band_send, band_recv,
):
    offsets, layers, rows, cells = panel_hbm.shape
    probes = res_hbm.shape[-1]
    chunks, part = blocks.shape[1], blocks.shape[3]
    band = cells // lats
    lat, lon = lax.axis_index("lat"), lax.axis_index("lon")
    period, source, order = route(offsets, lons)
    pair = 2 if lats % 2 == 0 else 1
    groups = lats // pair

    res_load = pltpu.make_async_copy(res_hbm, res, input_sem.at[0])
    nw_load = pltpu.make_async_copy(nw_hbm, nw, input_sem.at[1])
    res_load.start()
    nw_load.start()
    loads = {}
    for d in [0] + order:
        loads[d] = pltpu.make_async_copy(panel_hbm.at[d], panel.at[d], panel_sem.at[d])
        loads[d].start()

    def along(delta):
        return (lat, lax.rem(lon + (delta + lons), lons))

    def across(a, b):
        to = lax.rem(lat // pair + a, groups) * pair + lax.rem(lat % pair + b, pair)
        return (to, lon)

    partners = [(a, 0) for a in range(1, groups)] + [(0, b) for b in range(1, pair)]

    sends = [[] for _ in range(period)]
    senders = [set() for _ in range(period)]
    for q in range(period):
        for d in order:
            delta, held = source[q][d]
            sends[(q + delta) % period].append((-delta, held, d))
            senders[q].add(delta)

    def per_parity(action):
        for q in range(period):
            if period == 1:
                action(q)
            else:
                pl.when(lax.rem(lon, period) == q)(functools.partial(action, q))

    barrier = pltpu.get_barrier_semaphore()

    def greet(q):
        for delta in sorted(senders[q]):
            pl.semaphore_signal(barrier, inc=1, device_id=along(delta), device_id_type=MESH)

    per_parity(greet)
    for a, b in partners:
        pl.semaphore_signal(barrier, inc=1, device_id=across(a, b), device_id_type=MESH)

    res_load.wait()
    nw_load.wait()
    columns = res.shape[1]
    pieces = [
        nw[:, y : y + 1] * res[y].astype(jnp.float32) for y in range(rows // columns)
    ]
    weighted = jnp.concatenate(pieces, axis=0).T.astype(jnp.bfloat16)
    for c in range(chunks):
        blocks[0, c] = weighted[:, c * part : (c + 1) * part]

    def east(q, n, c):
        delta, held, d = sends[q][n]
        return pltpu.make_async_remote_copy(
            src_ref=blocks.at[held, c],
            dst_ref=blocks.at[d, c],
            send_sem=east_send.at[n, c],
            recv_sem=east_recv.at[d, c],
            device_id=along(delta),
            device_id_type=MESH,
        )

    def forward(held, cs):
        def action(q):
            for c in cs:
                for n, send in enumerate(sends[q]):
                    if send[1] == held:
                        east(q, n, c).start()

        per_parity(action)

    def arrive(d, c):
        pltpu.make_async_remote_copy(
            src_ref=blocks.at[d, c],
            dst_ref=blocks.at[d, c],
            send_sem=east_send.at[0, c],
            recv_sem=east_recv.at[d, c],
            device_id=along(1),
            device_id_type=MESH,
        ).wait_recv()

    pl.semaphore_wait(barrier, len(senders[0]) + len(partners))
    forward(0, range(chunks))

    def product(d, c, l, cols):
        return jnp.dot(
            blocks[d, c], panel[d, l, pl.ds(c * part, part), cols],
            preferred_element_type=jnp.float32,
        )

    def accumulate(d, cs, first):
        for l in range(layers):

            @pl.loop(0, lats)
            def _(b):
                cols = pl.ds(pl.multiple_of(b * band, band), band)
                value = None if first else total[l, :, cols]
                for c in cs:
                    more = product(d, c, l, cols)
                    value = more if value is None else value + more
                total[l, :, cols] = value

    loads[0].wait()
    accumulate(0, range(chunks), True)
    for d in order[:-1]:
        for c in range(chunks):
            arrive(d, c)
            forward(d, [c])
        loads[d].wait()
        accumulate(d, range(chunks), False)

    last = order[-1]
    loads[last].wait()
    for c in range(chunks - 1):
        arrive(last, c)
        accumulate(last, [c], False)
    arrive(last, chunks - 1)

    def finish(to):
        cols = pl.ds(pl.multiple_of(to * band, band), band)
        return [
            total[l, :, cols] + product(last, chunks - 1, l, cols) for l in range(layers)
        ]

    def inner(a, b):
        return pltpu.make_async_remote_copy(
            src_ref=chip_out.at[a, b - 1],
            dst_ref=chip_in.at[a, b - 1],
            send_sem=chip_send.at[a, b - 1],
            recv_sem=chip_recv.at[a, b - 1],
            device_id=across(0, b),
            device_id_type=MESH,
        )

    def outer(a):
        return pltpu.make_async_remote_copy(
            src_ref=band_out.at[a - 1],
            dst_ref=band_in.at[a - 1],
            send_sem=band_send.at[a - 1],
            recv_sem=band_recv.at[a - 1],
            device_id=across(a, 0),
            device_id_type=MESH,
        )

    def offer(a):
        for b in range(1, pair):
            for l, value in enumerate(finish(across(a, b)[0])):
                chip_out[a, b - 1, l] = value.astype(jnp.bfloat16)
            inner(a, b).start()

    def collect(a, values):
        for b in range(1, pair):
            inner(a, b).wait_recv()
            values = [
                value + chip_in[a, b - 1, l].astype(jnp.float32)
                for l, value in enumerate(values)
            ]
        return values

    steps = list(range(1, groups)) + [0]
    offer(steps[0])
    for n, a in enumerate(steps):
        mine = finish(across(a, 0)[0])
        if n + 1 < groups:
            offer(steps[n + 1])
        mine = collect(a, mine)
        if a > 0:
            for l, value in enumerate(mine):
                band_out[a - 1, l] = value.astype(jnp.bfloat16)
            outer(a).start()
    for a in range(1, groups):
        outer(a).wait_recv()
        mine = [
            value + band_in[a - 1, l].astype(jnp.float32) for l, value in enumerate(mine)
        ]
    for l, value in enumerate(mine):
        out_ref[l] = value.T.reshape(out_ref.shape[1:])

    def drain(q):
        for c in range(chunks):
            for n in range(len(sends[q])):
                east(q, n, c).wait_send()

    per_parity(drain)
    for a in range(groups):
        for b in range(1, pair):
            inner(a, b).wait_send()
        if a > 0:
            outer(a).wait_send()


def per_device(lats, lons, residual, noise_weights, kernel):
    offsets, layers, rows, cells = kernel.shape
    probes = residual.shape[2]
    band = cells // lats
    chunks = 2 if rows % 256 == 0 else 1
    pair = 2 if lats % 2 == 0 else 1
    groups = lats // pair
    inner, outer = max(pair - 1, 1), max(groups - 1, 1)
    remote = pl.BlockSpec(memory_space=pltpu.HBM)
    return pl.pallas_call(
        functools.partial(sweep, lats, lons),
        out_shape=jax.ShapeDtypeStruct(
            (layers, residual.shape[0], residual.shape[1], probes), jnp.float32
        ),
        in_specs=[remote, remote, remote],
        out_specs=pl.BlockSpec(memory_space=pltpu.VMEM),
        scratch_shapes=[
            pltpu.VMEM(residual.shape, jnp.bfloat16),
            pltpu.VMEM(noise_weights.shape[::-1], jnp.float32),
            pltpu.VMEM((offsets, layers, rows, cells), jnp.bfloat16),
            pltpu.VMEM((offsets, chunks, probes, rows // chunks), jnp.bfloat16),
            pltpu.VMEM((layers, probes, cells), jnp.float32),
            pltpu.VMEM((groups, inner, layers, probes, band), jnp.bfloat16),
            pltpu.VMEM((groups, inner, layers, probes, band), jnp.bfloat16),
            pltpu.VMEM((outer, layers, probes, band), jnp.bfloat16),
            pltpu.VMEM((outer, layers, probes, band), jnp.bfloat16),
            pltpu.SemaphoreType.DMA((2,)),
            pltpu.SemaphoreType.DMA((offsets,)),
            pltpu.SemaphoreType.DMA((2 * offsets, chunks)),
            pltpu.SemaphoreType.DMA((offsets, chunks)),
            pltpu.SemaphoreType.DMA((groups, inner)),
            pltpu.SemaphoreType.DMA((groups, inner)),
            pltpu.SemaphoreType.DMA((outer,)),
            pltpu.SemaphoreType.DMA((outer,)),
        ],
        compiler_params=pltpu.CompilerParams(
            collective_id=0, has_side_effects=True, vmem_limit_bytes=63 * 1024 * 1024
        ),
        cost_estimate=pl.CostEstimate(
            flops=2 * offsets * layers * rows * cells * probes,
            bytes_accessed=2 * offsets * layers * rows * cells,
            transcendentals=0,
        ),
    )(residual, noise_weights.T, kernel)


def solution(mesh):
    return jax.shard_map(
        functools.partial(per_device, mesh.shape["lat"], mesh.shape["lon"]),
        mesh=mesh,
        in_specs=(P("lat", "lon", None), P("lat", "lon"), P(None, None, "lat", None)),
        out_specs=P(None, "lat", "lon", None),
        check_vma=False,
    )
```

```python
import functools

import jax
import jax.numpy as jnp
from jax import lax
from jax.experimental import pallas as pl
from jax.experimental.pallas import tpu as pltpu
from jax.sharding import PartitionSpec as P

MESH = pl.DeviceIdType.MESH


def route(offsets, lons, chunks):
    direct = {d: (-d, 0) for d in range(1, offsets)}
    if lons % 2 or offsets < 3 or lons <= offsets:
        return 1, [[direct] * chunks], list(range(1, offsets))
    even, odd = [], []
    for c in range(chunks):
        even.append({**direct, 1: (1, 2)})
        odd.append(dict(direct))
        if offsets > 3:
            odd[c][3] = (-1, 2)
            if c % 2:
                even[c][3] = (1, offsets)
                odd[c][offsets] = (-4, 0)
    rest = [d for d in range(1, offsets) if d != 2]
    return 2, [even, odd], [2, offsets] + rest


def sweep(
    lats, lons, res_hbm, nw_hbm, panel_hbm, out_ref,
    res, nw, panel, blocks, total, outgoing, incoming, summed,
    input_sem, panel_sem, east_send, east_recv, band_send, band_recv,
):
    offsets, layers, rows, cells = panel_hbm.shape
    probes = res_hbm.shape[-1]
    chunks, part = outgoing.shape[0], outgoing.shape[3]
    band = cells // lats
    lat, lon = lax.axis_index("lat"), lax.axis_index("lon")
    period, source, order = route(offsets, lons, chunks)
    pair = 2 if lats % 2 == 0 else 1
    groups = lats // pair

    res_load = pltpu.make_async_copy(res_hbm, res, input_sem.at[0])
    nw_load = pltpu.make_async_copy(nw_hbm, nw, input_sem.at[1])
    res_load.start()
    nw_load.start()
    loads = {}
    for d in [0] + [d for d in order if d < offsets]:
        loads[d] = pltpu.make_async_copy(panel_hbm.at[d], panel.at[d], panel_sem.at[d])
        loads[d].start()

    def along(delta):
        return (lat, lax.rem(lon + (delta + lons), lons))

    def across(a, b):
        to = lax.rem(lat // pair + a, groups) * pair + lax.rem(lat % pair + b, pair)
        return (to, lon)

    partners = [(a, b) for a in range(groups - 1, -1, -1) for b in range(pair)][: lats]
    partners = [ab for ab in partners if ab != (0, 0)]

    sends = [[[] for _ in range(chunks)] for _ in range(period)]
    senders = [set() for _ in range(period)]
    for q in range(period):
        for c in range(chunks):
            for d in order:
                if d in source[q][c]:
                    delta, held = source[q][c][d]
                    sends[(q + delta) % period][c].append((-delta, held, d))
                    senders[q].add(delta)
    for lists in sends:
        for some in lists:
            some.sort(key=lambda send: order.index(send[2]))
    receivers = [{send[0] for c in range(chunks) for send in sends[q][c]} for q in range(period)]

    def per_parity(action):
        for q in range(period):
            if period == 1:
                action(q)
            else:
                pl.when(lax.rem(lon, period) == q)(functools.partial(action, q))

    barrier = pltpu.get_barrier_semaphore()

    def greet(q):
        for delta in sorted(senders[q]):
            pl.semaphore_signal(barrier, inc=1, device_id=along(delta), device_id_type=MESH)

    per_parity(greet)
    for a, b in partners:
        pl.semaphore_signal(barrier, inc=1, device_id=across(a, b), device_id_type=MESH)

    res_load.wait()
    nw_load.wait()
    columns = res.shape[1]
    pieces = [
        nw[:, y : y + 1] * res[y].astype(jnp.float32) for y in range(rows // columns)
    ]
    blocks[0] = jnp.concatenate(pieces, axis=0).T.astype(jnp.bfloat16)

    def chunk(c):
        return pl.ds(c * part, part)

    def east(q, n, c):
        delta, held, d = sends[q][c][n]
        return pltpu.make_async_remote_copy(
            src_ref=blocks.at[held, chunk(c)],
            dst_ref=blocks.at[d, chunk(c)],
            send_sem=east_send.at[n, c],
            recv_sem=east_recv.at[d, c],
            device_id=along(delta),
            device_id_type=MESH,
        )

    def outgoing_of(q, held, c):
        return [n for n, send in enumerate(sends[q][c]) if send[1] == held]

    def forward(held, c):
        def action(q):
            for n in outgoing_of(q, held, c):
                east(q, n, c).start()

        per_parity(action)

    def follow(c):
        def action(q):
            before, now = outgoing_of(q, 0, c - 1), outgoing_of(q, 0, c)
            for n in before:
                east(q, n, c - 1).wait_send()
                if now:
                    east(q, now.pop(0), c).start()
            for n in now:
                east(q, n, c).start()

        per_parity(action)

    def arrive(d, c):
        pltpu.make_async_remote_copy(
            src_ref=blocks.at[d, chunk(c)],
            dst_ref=blocks.at[d, chunk(c)],
            send_sem=east_send.at[0, c],
            recv_sem=east_recv.at[d, c],
            device_id=along(1),
            device_id_type=MESH,
        ).wait_recv()

    def admit(q):
        pl.semaphore_wait(barrier, len(receivers[q]) + len(partners))

    per_parity(admit)
    forward(0, 0)
    for c in range(1, chunks):
        follow(c)

    def accumulate(d, first):
        loads[d].wait()
        for l in range(layers):

            @pl.loop(0, lats)
            def _(b):
                cols = pl.ds(pl.multiple_of(b * band, band), band)
                value = jnp.dot(
                    blocks[d], panel[d, l, :, cols], preferred_element_type=jnp.float32
                )
                total[l, :, cols] = value if first else total[l, :, cols] + value

    accumulate(0, True)
    def relay(d):
        def action(q):
            for c in range(chunks):
                if d in source[q][c]:
                    arrive(d, c)
                    for n in outgoing_of(q, d, c):
                        east(q, n, c).start()

        per_parity(action)

    for n, d in enumerate(order[:-1]):
        relay(d)
        if d == offsets:
            accumulate(order[n - 1], False)
        elif order[n + 1] != offsets:
            accumulate(d, False)

    last = order[-1]
    loads[last].wait()

    def finish(c, to):
        cols = pl.ds(pl.multiple_of(to * band, band), band)
        return [
            total[l, chunk(c), cols]
            + jnp.dot(
                blocks[last, chunk(c)], panel[last, l, :, cols],
                preferred_element_type=jnp.float32,
            )
            for l in range(layers)
        ]

    sent = {}
    for c in range(chunks):
        arrive(last, c)
        for n, (a, b) in enumerate(partners):
            to = across(a, b)
            for l, value in enumerate(finish(c, to[0])):
                outgoing[c, n, l] = value.astype(jnp.bfloat16)
            sent[c, n] = pltpu.make_async_remote_copy(
                src_ref=outgoing.at[c, n],
                dst_ref=incoming.at[c, n],
                send_sem=band_send.at[c, n],
                recv_sem=band_recv.at[c, n],
                device_id=to,
                device_id_type=MESH,
            )
            sent[c, n].start()
        for l, value in enumerate(finish(c, lat)):
            summed[l, chunk(c)] = value
    for c in range(chunks):
        for n in reversed(range(len(partners))):
            sent[c, n].wait_recv()
        for l in range(layers):
            value = summed[l, chunk(c)]
            for n in range(len(partners)):
                value = value + incoming[c, n, l].astype(jnp.float32)
            summed[l, chunk(c)] = value
    for l in range(layers):
        out_ref[l] = summed[l].T.reshape(out_ref.shape[1:])

    def drain(q):
        for c in range(chunks):
            for n, send in enumerate(sends[q][c]):
                if send[1] > 0 or c == chunks - 1:
                    east(q, n, c).wait_send()

    per_parity(drain)
    for copy in sent.values():
        copy.wait_send()


def per_device(lats, lons, residual, noise_weights, kernel):
    offsets, layers, rows, cells = kernel.shape
    probes = residual.shape[2]
    band = cells // lats
    chunks = 2 if probes % 32 == 0 else 1
    part = probes // chunks
    remote = pl.BlockSpec(memory_space=pltpu.HBM)
    return pl.pallas_call(
        functools.partial(sweep, lats, lons),
        out_shape=jax.ShapeDtypeStruct(
            (layers, residual.shape[0], residual.shape[1], probes), jnp.float32
        ),
        in_specs=[remote, remote, remote],
        out_specs=pl.BlockSpec(memory_space=pltpu.VMEM),
        scratch_shapes=[
            pltpu.VMEM(residual.shape, jnp.bfloat16),
            pltpu.VMEM(noise_weights.shape[::-1], jnp.float32),
            pltpu.VMEM((offsets, layers, rows, cells), jnp.bfloat16),
            pltpu.VMEM((offsets + 1, probes, rows), jnp.bfloat16),
            pltpu.VMEM((layers, probes, cells), jnp.float32),
            pltpu.VMEM((chunks, lats - 1, layers, part, band), jnp.bfloat16),
            pltpu.VMEM((chunks, lats - 1, layers, part, band), jnp.bfloat16),
            pltpu.VMEM((layers, probes, band), jnp.float32),
            pltpu.SemaphoreType.DMA((2,)),
            pltpu.SemaphoreType.DMA((offsets,)),
            pltpu.SemaphoreType.DMA((2 * offsets, chunks)),
            pltpu.SemaphoreType.DMA((offsets + 1, chunks)),
            pltpu.SemaphoreType.DMA((chunks, lats - 1)),
            pltpu.SemaphoreType.DMA((chunks, lats - 1)),
        ],
        compiler_params=pltpu.CompilerParams(
            collective_id=0, has_side_effects=True, vmem_limit_bytes=63 * 1024 * 1024
        ),
        cost_estimate=pl.CostEstimate(
            flops=2 * offsets * layers * rows * cells * probes,
            bytes_accessed=2 * offsets * layers * rows * cells,
            transcendentals=0,
        ),
    )(residual, noise_weights.T, kernel)


def solution(mesh):
    return jax.shard_map(
        functools.partial(per_device, mesh.shape["lat"], mesh.shape["lon"]),
        mesh=mesh,
        in_specs=(P("lat", "lon", None), P("lat", "lon"), P(None, None, "lat", None)),
        out_specs=P(None, "lat", "lon", None),
        check_vma=False,
    )
```

```python
import functools

import jax
import jax.numpy as jnp
from jax import lax
from jax.experimental import pallas as pl
from jax.experimental.pallas import tpu as pltpu
from jax.sharding import PartitionSpec as P

MESH = pl.DeviceIdType.MESH


def route(offsets, lons, chunks):
    direct = {d: (-d, 0) for d in range(1, offsets)}
    if lons % 2 or offsets < 3 or lons <= offsets:
        return 1, [[direct] * chunks], list(range(1, offsets))
    even, odd = [], []
    for c in range(chunks):
        even.append({**direct, 1: (1, 2)})
        odd.append(dict(direct))
        if offsets > 3:
            odd[c][3] = (-1, 2)
            if c % 2:
                even[c][offsets] = (1, 0)
                even[c][3] = (-4, offsets)
            else:
                odd[c][offsets] = (-4, 0)
                even[c][3] = (1, offsets)
    rest = [d for d in range(1, offsets) if d != 2]
    return 2, [even, odd], [2, offsets] + rest


def sweep(
    lats, lons, res_hbm, nw_hbm, panel_hbm, out_ref,
    res, nw, panel, blocks, total, outgoing, incoming, summed,
    input_sem, panel_sem, east_send, east_recv, band_send, band_recv,
):
    offsets, layers, rows, cells = panel_hbm.shape
    probes = res_hbm.shape[-1]
    chunks, part = outgoing.shape[0], outgoing.shape[3]
    band = cells // lats
    lat, lon = lax.axis_index("lat"), lax.axis_index("lon")
    period, source, order = route(offsets, lons, chunks)
    pair = 2 if lats % 2 == 0 else 1
    groups = lats // pair

    res_load = pltpu.make_async_copy(res_hbm, res, input_sem.at[0])
    nw_load = pltpu.make_async_copy(nw_hbm, nw, input_sem.at[1])
    res_load.start()
    nw_load.start()
    loads = {}
    for d in [0] + [d for d in order if d < offsets]:
        loads[d] = pltpu.make_async_copy(panel_hbm.at[d], panel.at[d], panel_sem.at[d])
        loads[d].start()

    def along(delta):
        return (lat, lax.rem(lon + (delta + lons), lons))

    def across(a, b):
        to = lax.rem(lat // pair + a, groups) * pair + lax.rem(lat % pair + b, pair)
        return (to, lon)

    partners = [(a, b) for a in range(groups - 1, -1, -1) for b in range(pair)][: lats]
    partners = [ab for ab in partners if ab != (0, 0)]

    sends = [[[] for _ in range(chunks)] for _ in range(period)]
    senders = [set() for _ in range(period)]
    for q in range(period):
        for c in range(chunks):
            for d in order:
                if d in source[q][c]:
                    delta, held = source[q][c][d]
                    sends[(q + delta) % period][c].append((-delta, held, d))
                    senders[q].add(delta)
    for lists in sends:
        for some in lists:
            some.sort(key=lambda send: order.index(send[2]))
    receivers = [{send[0] for c in range(chunks) for send in sends[q][c]} for q in range(period)]

    def per_parity(action):
        for q in range(period):
            if period == 1:
                action(q)
            else:
                pl.when(lax.rem(lon, period) == q)(functools.partial(action, q))

    barrier = pltpu.get_barrier_semaphore()

    def greet(q):
        for delta in sorted(senders[q]):
            pl.semaphore_signal(barrier, inc=1, device_id=along(delta), device_id_type=MESH)

    per_parity(greet)
    for a, b in partners:
        pl.semaphore_signal(barrier, inc=1, device_id=across(a, b), device_id_type=MESH)

    res_load.wait()
    nw_load.wait()
    columns = res.shape[1]
    pieces = [
        nw[:, y : y + 1] * res[y].astype(jnp.float32) for y in range(rows // columns)
    ]
    blocks[0] = jnp.concatenate(pieces, axis=0).T.astype(jnp.bfloat16)

    def chunk(c):
        return pl.ds(c * part, part)

    def east(q, n, c):
        delta, held, d = sends[q][c][n]
        return pltpu.make_async_remote_copy(
            src_ref=blocks.at[held, chunk(c)],
            dst_ref=blocks.at[d, chunk(c)],
            send_sem=east_send.at[n, c],
            recv_sem=east_recv.at[d, c],
            device_id=along(delta),
            device_id_type=MESH,
        )

    def outgoing_of(q, held, c):
        return [n for n, send in enumerate(sends[q][c]) if send[1] == held]

    def forward(held, c):
        def action(q):
            for n in outgoing_of(q, held, c):
                east(q, n, c).start()

        per_parity(action)

    def arrive(d, c):
        pltpu.make_async_remote_copy(
            src_ref=blocks.at[d, chunk(c)],
            dst_ref=blocks.at[d, chunk(c)],
            send_sem=east_send.at[0, c],
            recv_sem=east_recv.at[d, c],
            device_id=along(1),
            device_id_type=MESH,
        ).wait_recv()

    def admit(q):
        pl.semaphore_wait(barrier, len(receivers[q]) + len(partners))

    per_parity(admit)
    for c in range(chunks):
        forward(0, c)

    def accumulate(d, first):
        loads[d].wait()
        for l in range(layers):

            @pl.loop(0, lats)
            def _(b):
                cols = pl.ds(pl.multiple_of(b * band, band), band)
                value = jnp.dot(
                    blocks[d], panel[d, l, :, cols], preferred_element_type=jnp.float32
                )
                total[l, :, cols] = value if first else total[l, :, cols] + value

    accumulate(0, True)
    def relay(d):
        def action(q):
            for c in range(chunks):
                if d in source[q][c]:
                    arrive(d, c)
                    for n in outgoing_of(q, d, c):
                        east(q, n, c).start()

        per_parity(action)

    for n, d in enumerate(order[:-1]):
        relay(d)
        if d == offsets:
            accumulate(order[n - 1], False)
        elif order[n + 1] != offsets:
            accumulate(d, False)

    last = order[-1]
    loads[last].wait()

    def finish(c, to):
        cols = pl.ds(pl.multiple_of(to * band, band), band)
        return [
            total[l, chunk(c), cols]
            + jnp.dot(
                blocks[last, chunk(c)], panel[last, l, :, cols],
                preferred_element_type=jnp.float32,
            )
            for l in range(layers)
        ]

    sent = {}
    for c in range(chunks):
        arrive(last, c)
        for n, (a, b) in enumerate(partners):
            to = across(a, b)
            for l, value in enumerate(finish(c, to[0])):
                outgoing[c, n, l] = value.astype(jnp.bfloat16)
            sent[c, n] = pltpu.make_async_remote_copy(
                src_ref=outgoing.at[c, n],
                dst_ref=incoming.at[c, n],
                send_sem=band_send.at[c, n],
                recv_sem=band_recv.at[c, n],
                device_id=to,
                device_id_type=MESH,
            )
            sent[c, n].start()
        for l, value in enumerate(finish(c, lat)):
            summed[l, chunk(c)] = value
    for c in range(chunks):
        for n in reversed(range(len(partners))):
            sent[c, n].wait_recv()
        for l in range(layers):
            value = summed[l, chunk(c)]
            for n in range(len(partners)):
                value = value + incoming[c, n, l].astype(jnp.float32)
            summed[l, chunk(c)] = value
    for l in range(layers):
        out_ref[l] = summed[l].T.reshape(out_ref.shape[1:])

    def drain(q):
        for c in range(chunks):
            for n in range(len(sends[q][c])):
                east(q, n, c).wait_send()

    per_parity(drain)
    for copy in sent.values():
        copy.wait_send()


def per_device(lats, lons, residual, noise_weights, kernel):
    offsets, layers, rows, cells = kernel.shape
    probes = residual.shape[2]
    band = cells // lats
    chunks = 2 if probes % 32 == 0 else 1
    part = probes // chunks
    remote = pl.BlockSpec(memory_space=pltpu.HBM)
    return pl.pallas_call(
        functools.partial(sweep, lats, lons),
        out_shape=jax.ShapeDtypeStruct(
            (layers, residual.shape[0], residual.shape[1], probes), jnp.float32
        ),
        in_specs=[remote, remote, remote],
        out_specs=pl.BlockSpec(memory_space=pltpu.VMEM),
        scratch_shapes=[
            pltpu.VMEM(residual.shape, jnp.bfloat16),
            pltpu.VMEM(noise_weights.shape[::-1], jnp.float32),
            pltpu.VMEM((offsets, layers, rows, cells), jnp.bfloat16),
            pltpu.VMEM((offsets + 1, probes, rows), jnp.bfloat16),
            pltpu.VMEM((layers, probes, cells), jnp.float32),
            pltpu.VMEM((chunks, lats - 1, layers, part, band), jnp.bfloat16),
            pltpu.VMEM((chunks, lats - 1, layers, part, band), jnp.bfloat16),
            pltpu.VMEM((layers, probes, band), jnp.float32),
            pltpu.SemaphoreType.DMA((2,)),
            pltpu.SemaphoreType.DMA((offsets,)),
            pltpu.SemaphoreType.DMA((2 * offsets, chunks)),
            pltpu.SemaphoreType.DMA((offsets + 1, chunks)),
            pltpu.SemaphoreType.DMA((chunks, lats - 1)),
            pltpu.SemaphoreType.DMA((chunks, lats - 1)),
        ],
        compiler_params=pltpu.CompilerParams(
            collective_id=0, has_side_effects=True, vmem_limit_bytes=48 * 1024 * 1024
        ),
        cost_estimate=pl.CostEstimate(
            flops=2 * offsets * layers * rows * cells * probes,
            bytes_accessed=2 * offsets * layers * rows * cells,
            transcendentals=0,
        ),
    )(residual, noise_weights.T, kernel)


def solution(mesh):
    return jax.shard_map(
        functools.partial(per_device, mesh.shape["lat"], mesh.shape["lon"]),
        mesh=mesh,
        in_specs=(P("lat", "lon", None), P("lat", "lon"), P(None, None, "lat", None)),
        out_specs=P(None, "lat", "lon", None),
        check_vma=False,
    )
```

```python
import functools

import jax
import jax.numpy as jnp
from jax import lax
from jax.experimental import pallas as pl
from jax.experimental.pallas import tpu as pltpu
from jax.sharding import PartitionSpec as P

MESH = pl.DeviceIdType.MESH


def route(offsets, lons, chunks):
    direct = {d: (-d, 0) for d in range(1, offsets)}
    if lons % 2 or offsets < 3 or lons <= offsets:
        return 1, [[direct] * chunks], list(range(1, offsets))
    even, odd = [], []
    for c in range(chunks):
        even.append({**direct, 1: (1, 2)})
        odd.append(dict(direct))
        if offsets > 3:
            odd[c][3] = (-1, 2)
            if c % 2:
                even[c][offsets] = (1, 0)
                even[c][3] = (-4, offsets)
            else:
                odd[c][offsets] = (-4, 0)
                even[c][3] = (1, offsets)
    rest = [d for d in range(1, offsets) if d != 2]
    return 2, [even, odd], [2, offsets] + rest


def sweep(
    lats, lons, res_hbm, nw_hbm, panel_hbm, out_ref,
    res, nw, panel, blocks, total, outgoing, incoming, summed,
    input_sem, panel_sem, east_send, east_recv, band_send, band_recv,
):
    offsets, layers, rows, cells = panel_hbm.shape
    probes = res_hbm.shape[-1]
    chunks, part = outgoing.shape[0], outgoing.shape[3]
    band = cells // lats
    lat, lon = lax.axis_index("lat"), lax.axis_index("lon")
    period, source, order = route(offsets, lons, chunks)
    pair = 2 if lats % 2 == 0 else 1
    groups = lats // pair

    res_load = pltpu.make_async_copy(res_hbm, res, input_sem.at[0])
    nw_load = pltpu.make_async_copy(nw_hbm, nw, input_sem.at[1])
    res_load.start()
    nw_load.start()
    loads = {}
    for d in [0] + [d for d in order if d < offsets]:
        loads[d] = pltpu.make_async_copy(panel_hbm.at[d], panel.at[d], panel_sem.at[d])
        loads[d].start()

    def along(delta):
        return (lat, lax.rem(lon + (delta + lons), lons))

    def across(a, b):
        to = lax.rem(lat // pair + a, groups) * pair + lax.rem(lat % pair + b, pair)
        return (to, lon)

    partners = [(a, b) for a in range(groups - 1, -1, -1) for b in range(pair)][: lats]
    partners = [ab for ab in partners if ab != (0, 0)]

    sends = [[[] for _ in range(chunks)] for _ in range(period)]
    senders = [set() for _ in range(period)]
    for q in range(period):
        for c in range(chunks):
            for d in order:
                if d in source[q][c]:
                    delta, held = source[q][c][d]
                    sends[(q + delta) % period][c].append((-delta, held, d))
                    senders[q].add(delta)
    for lists in sends:
        for some in lists:
            some.sort(key=lambda send: order.index(send[2]))
    receivers = [{send[0] for c in range(chunks) for send in sends[q][c]} for q in range(period)]

    def per_parity(action):
        for q in range(period):
            if period == 1:
                action(q)
            else:
                pl.when(lax.rem(lon, period) == q)(functools.partial(action, q))

    barrier = pltpu.get_barrier_semaphore()

    def greet(q):
        for delta in sorted(senders[q]):
            pl.semaphore_signal(barrier, inc=1, device_id=along(delta), device_id_type=MESH)

    per_parity(greet)
    for a, b in partners:
        pl.semaphore_signal(barrier, inc=1, device_id=across(a, b), device_id_type=MESH)

    res_load.wait()
    nw_load.wait()
    columns = res.shape[1]
    pieces = [
        nw[:, y : y + 1] * res[y].astype(jnp.float32) for y in range(rows // columns)
    ]
    blocks[0] = jnp.concatenate(pieces, axis=0).T.astype(jnp.bfloat16)

    def chunk(c):
        return pl.ds(c * part, part)

    def east(q, n, c):
        delta, held, d = sends[q][c][n]
        return pltpu.make_async_remote_copy(
            src_ref=blocks.at[held, chunk(c)],
            dst_ref=blocks.at[d, chunk(c)],
            send_sem=east_send.at[n, c],
            recv_sem=east_recv.at[d, c],
            device_id=along(delta),
            device_id_type=MESH,
        )

    def outgoing_of(q, held, c):
        return [n for n, send in enumerate(sends[q][c]) if send[1] == held]

    def forward(held, c):
        def action(q):
            for n in outgoing_of(q, held, c):
                east(q, n, c).start()

        per_parity(action)

    def arrive(d, c):
        pltpu.make_async_remote_copy(
            src_ref=blocks.at[d, chunk(c)],
            dst_ref=blocks.at[d, chunk(c)],
            send_sem=east_send.at[0, c],
            recv_sem=east_recv.at[d, c],
            device_id=along(1),
            device_id_type=MESH,
        ).wait_recv()

    def admit(q):
        pl.semaphore_wait(barrier, len(receivers[q]) + len(partners))

    per_parity(admit)
    for c in range(chunks):
        forward(0, c)

    def accumulate(d, first):
        loads[d].wait()
        for l in range(layers):

            @pl.loop(0, lats)
            def _(b):
                cols = pl.ds(pl.multiple_of(b * band, band), band)
                value = jnp.dot(
                    blocks[d], panel[d, l, :, cols], preferred_element_type=jnp.float32
                )
                total[l, :, cols] = value if first else total[l, :, cols] + value

    accumulate(0, True)
    def relay(d):
        def action(q):
            for c in range(chunks):
                if d in source[q][c]:
                    arrive(d, c)
                    for n in outgoing_of(q, d, c):
                        east(q, n, c).start()

        per_parity(action)

    for n, d in enumerate(order[:-1]):
        relay(d)
        if d == offsets:
            accumulate(order[n - 1], False)
        elif order[n + 1] != offsets:
            accumulate(d, False)

    last = order[-1]
    loads[last].wait()

    def band_copy(c, n):
        return pltpu.make_async_remote_copy(
            src_ref=outgoing.at[c, n],
            dst_ref=incoming.at[c, n],
            send_sem=band_send.at[c, n],
            recv_sem=band_recv.at[c, n],
            device_id=across(groups - 1 - n // pair, pair - 1 - n % pair),
            device_id_type=MESH,
        )

    @pl.loop(0, chunks)
    def _(c):
        arrive(last, c)
        here = pl.ds(pl.multiple_of(c * part, part), part)

        @pl.loop(0, lats)
        def _(n):
            to = across(groups - 1 - n // pair, pair - 1 - n % pair)[0]
            cols = pl.ds(pl.multiple_of(to * band, band), band)
            for l in range(layers):
                value = total[l, here, cols] + jnp.dot(
                    blocks[last, here], panel[last, l, :, cols],
                    preferred_element_type=jnp.float32,
                )
                outgoing[c, n, l] = value.astype(jnp.bfloat16)
                summed[l, here] = value

            @pl.when(n < lats - 1)
            def _():
                band_copy(c, n).start()

    @pl.loop(0, chunks)
    def _(c):
        here = pl.ds(pl.multiple_of(c * part, part), part)
        for n in range(lats - 1):
            band_copy(c, n).wait_recv()
        for l in range(layers):
            value = summed[l, here]
            for n in range(lats - 1):
                value = value + incoming[c, n, l].astype(jnp.float32)
            summed[l, here] = value

    for l in range(layers):
        out_ref[l] = summed[l].T.reshape(out_ref.shape[1:])

    def drain(q):
        for c in range(chunks):
            for n in range(len(sends[q][c])):
                east(q, n, c).wait_send()

    per_parity(drain)

    @pl.loop(0, chunks)
    def _(c):
        @pl.loop(0, lats - 1)
        def _(n):
            band_copy(c, n).wait_send()


def per_device(lats, lons, residual, noise_weights, kernel):
    offsets, layers, rows, cells = kernel.shape
    probes = residual.shape[2]
    band = cells // lats
    chunks = 2 if probes % 32 == 0 else 1
    part = probes // chunks
    remote = pl.BlockSpec(memory_space=pltpu.HBM)
    return pl.pallas_call(
        functools.partial(sweep, lats, lons),
        out_shape=jax.ShapeDtypeStruct(
            (layers, residual.shape[0], residual.shape[1], probes), jnp.float32
        ),
        in_specs=[remote, remote, remote],
        out_specs=pl.BlockSpec(memory_space=pltpu.VMEM),
        scratch_shapes=[
            pltpu.VMEM(residual.shape, jnp.bfloat16),
            pltpu.VMEM(noise_weights.shape[::-1], jnp.float32),
            pltpu.VMEM((offsets, layers, rows, cells), jnp.bfloat16),
            pltpu.VMEM((offsets + 1, probes, rows), jnp.bfloat16),
            pltpu.VMEM((layers, probes, cells), jnp.float32),
            pltpu.VMEM((chunks, lats, layers, part, band), jnp.bfloat16),
            pltpu.VMEM((chunks, lats - 1, layers, part, band), jnp.bfloat16),
            pltpu.VMEM((layers, probes, band), jnp.float32),
            pltpu.SemaphoreType.DMA((2,)),
            pltpu.SemaphoreType.DMA((offsets,)),
            pltpu.SemaphoreType.DMA((2 * offsets, chunks)),
            pltpu.SemaphoreType.DMA((offsets + 1, chunks)),
            pltpu.SemaphoreType.DMA((chunks, lats - 1)),
            pltpu.SemaphoreType.DMA((chunks, lats - 1)),
        ],
        compiler_params=pltpu.CompilerParams(
            collective_id=0, has_side_effects=True, vmem_limit_bytes=63 * 1024 * 1024
        ),
        cost_estimate=pl.CostEstimate(
            flops=2 * offsets * layers * rows * cells * probes,
            bytes_accessed=2 * offsets * layers * rows * cells,
            transcendentals=0,
        ),
    )(residual, noise_weights.T, kernel)


def solution(mesh):
    return jax.shard_map(
        functools.partial(per_device, mesh.shape["lat"], mesh.shape["lon"]),
        mesh=mesh,
        in_specs=(P("lat", "lon", None), P("lat", "lon"), P(None, None, "lat", None)),
        out_specs=P(None, "lat", "lon", None),
        check_vma=False,
    )
```

```python
import functools

import jax
import jax.numpy as jnp
from jax import lax
from jax.experimental import pallas as pl
from jax.experimental.pallas import tpu as pltpu
from jax.sharding import PartitionSpec as P

MESH = pl.DeviceIdType.MESH


def route(offsets, lons, chunks):
    direct = {d: (-d, 0) for d in range(1, offsets)}
    if lons % 2 or offsets < 3 or lons <= offsets:
        return 1, [[direct] * chunks], list(range(1, offsets))
    even, odd = [], []
    for c in range(chunks):
        even.append({**direct, 1: (1, 2)})
        odd.append(dict(direct))
        if offsets > 3:
            odd[c][3] = (-1, 2)
            if c % 2:
                even[c][offsets] = (1, 0)
                even[c][3] = (-4, offsets)
            else:
                odd[c][offsets] = (-4, 0)
                even[c][3] = (1, offsets)
    rest = [d for d in range(1, offsets) if d != 2]
    return 2, [even, odd], [2, offsets] + rest


def sweep(
    lats, lons, res_hbm, nw_hbm, panel_hbm, out_ref,
    res, nw, panel, blocks, total, outgoing, incoming, summed,
    input_sem, panel_sem, east_send, east_recv, band_send, band_recv,
):
    offsets, layers, rows, cells = panel_hbm.shape
    probes = res_hbm.shape[-1]
    chunks, part = outgoing.shape[0], outgoing.shape[3]
    band = cells // lats
    lat, lon = lax.axis_index("lat"), lax.axis_index("lon")
    period, source, order = route(offsets, lons, chunks)
    pair = 2 if lats % 2 == 0 else 1
    groups = lats // pair

    res_load = pltpu.make_async_copy(res_hbm, res, input_sem.at[0])
    nw_load = pltpu.make_async_copy(nw_hbm, nw, input_sem.at[1])
    res_load.start()
    nw_load.start()
    loads = {}
    for d in [0] + [d for d in order if d < offsets]:
        loads[d] = pltpu.make_async_copy(panel_hbm.at[d], panel.at[d], panel_sem.at[d])
        loads[d].start()

    def along(delta):
        return (lat, lax.rem(lon + (delta + lons), lons))

    def across(a, b):
        to = lax.rem(lat // pair + a, groups) * pair + lax.rem(lat % pair + b, pair)
        return (to, lon)

    partners = [(a, b) for a in range(groups - 1, -1, -1) for b in range(pair)][: lats]
    partners = [ab for ab in partners if ab != (0, 0)]

    sends = [[[] for _ in range(chunks)] for _ in range(period)]
    senders = [set() for _ in range(period)]
    for q in range(period):
        for c in range(chunks):
            for d in order:
                if d in source[q][c]:
                    delta, held = source[q][c][d]
                    sends[(q + delta) % period][c].append((-delta, held, d))
                    senders[q].add(delta)
    for lists in sends:
        for some in lists:
            some.sort(key=lambda send: order.index(send[2]))
    receivers = [{send[0] for c in range(chunks) for send in sends[q][c]} for q in range(period)]

    def per_parity(action):
        for q in range(period):
            if period == 1:
                action(q)
            else:
                pl.when(lax.rem(lon, period) == q)(functools.partial(action, q))

    barrier = pltpu.get_barrier_semaphore()

    def greet(q):
        for delta in sorted(senders[q]):
            pl.semaphore_signal(barrier, inc=1, device_id=along(delta), device_id_type=MESH)

    per_parity(greet)
    for a, b in partners:
        pl.semaphore_signal(barrier, inc=1, device_id=across(a, b), device_id_type=MESH)

    res_load.wait()
    nw_load.wait()
    columns = res.shape[1]
    pieces = [
        nw[:, y : y + 1] * res[y].astype(jnp.float32) for y in range(rows // columns)
    ]
    blocks[0] = jnp.concatenate(pieces, axis=0).T.astype(jnp.bfloat16)

    def chunk(c):
        return pl.ds(c * part, part)

    def east(q, n, c):
        delta, held, d = sends[q][c][n]
        return pltpu.make_async_remote_copy(
            src_ref=blocks.at[held, chunk(c)],
            dst_ref=blocks.at[d, chunk(c)],
            send_sem=east_send.at[n, c],
            recv_sem=east_recv.at[d, c],
            device_id=along(delta),
            device_id_type=MESH,
        )

    def outgoing_of(q, held, c):
        return [n for n, send in enumerate(sends[q][c]) if send[1] == held]

    def forward(held, c):
        def action(q):
            for n in outgoing_of(q, held, c):
                east(q, n, c).start()

        per_parity(action)

    def arrive(d, c):
        pltpu.make_async_remote_copy(
            src_ref=blocks.at[d, chunk(c)],
            dst_ref=blocks.at[d, chunk(c)],
            send_sem=east_send.at[0, c],
            recv_sem=east_recv.at[d, c],
            device_id=along(1),
            device_id_type=MESH,
        ).wait_recv()

    def admit(q):
        pl.semaphore_wait(barrier, len(receivers[q]) + len(partners))

    per_parity(admit)
    forward(0, 0)

    def accumulate(d, first):
        loads[d].wait()
        for l in range(layers):
            for b in range(lats):
                cols = pl.ds(b * band, band)
                value = jnp.dot(
                    blocks[d], panel[d, l, :, cols], preferred_element_type=jnp.float32
                )
                total[l, :, cols] = value if first else total[l, :, cols] + value

    accumulate(0, True)

    def follow(c):
        def action(q):
            before, now = outgoing_of(q, 0, c - 1), outgoing_of(q, 0, c)
            for n in before:
                east(q, n, c - 1).wait_send()
                if now:
                    east(q, now.pop(0), c).start()
            for n in now:
                east(q, n, c).start()

        per_parity(action)

    for c in range(1, chunks):
        follow(c)
    def relay(d):
        def action(q):
            for c in range(chunks):
                if d in source[q][c]:
                    arrive(d, c)
                    for n in outgoing_of(q, d, c):
                        east(q, n, c).start()

        per_parity(action)

    for n, d in enumerate(order[:-1]):
        relay(d)
        if d == offsets:
            accumulate(order[n - 1], False)
        elif order[n + 1] != offsets:
            accumulate(d, False)

    last = order[-1]
    loads[last].wait()

    def finish(c, to):
        cols = pl.ds(pl.multiple_of(to * band, band), band)
        return [
            total[l, chunk(c), cols]
            + jnp.dot(
                blocks[last, chunk(c)], panel[last, l, :, cols],
                preferred_element_type=jnp.float32,
            )
            for l in range(layers)
        ]

    sent = {}
    for c in range(chunks):
        arrive(last, c)
        for n, (a, b) in enumerate(partners):
            to = across(a, b)
            for l, value in enumerate(finish(c, to[0])):
                outgoing[c, n, l] = value.astype(jnp.bfloat16)
            sent[c, n] = pltpu.make_async_remote_copy(
                src_ref=outgoing.at[c, n],
                dst_ref=incoming.at[c, n],
                send_sem=band_send.at[c, n],
                recv_sem=band_recv.at[c, n],
                device_id=to,
                device_id_type=MESH,
            )
            sent[c, n].start()
        for l, value in enumerate(finish(c, lat)):
            summed[l, chunk(c)] = value
    for c in range(chunks):
        for n in reversed(range(len(partners))):
            sent[c, n].wait_recv()
        for l in range(layers):
            value = summed[l, chunk(c)]
            for n in range(len(partners)):
                value = value + incoming[c, n, l].astype(jnp.float32)
            summed[l, chunk(c)] = value
    for l in range(layers):
        out_ref[l] = summed[l].T.reshape(out_ref.shape[1:])

    def drain(q):
        for c in range(chunks):
            for n, send in enumerate(sends[q][c]):
                if send[1] > 0 or c == chunks - 1:
                    east(q, n, c).wait_send()

    per_parity(drain)
    for copy in sent.values():
        copy.wait_send()


def per_device(lats, lons, residual, noise_weights, kernel):
    offsets, layers, rows, cells = kernel.shape
    probes = residual.shape[2]
    band = cells // lats
    chunks = 2 if probes % 32 == 0 else 1
    part = probes // chunks
    remote = pl.BlockSpec(memory_space=pltpu.HBM)
    return pl.pallas_call(
        functools.partial(sweep, lats, lons),
        out_shape=jax.ShapeDtypeStruct(
            (layers, residual.shape[0], residual.shape[1], probes), jnp.float32
        ),
        in_specs=[remote, remote, remote],
        out_specs=pl.BlockSpec(memory_space=pltpu.VMEM),
        scratch_shapes=[
            pltpu.VMEM(residual.shape, jnp.bfloat16),
            pltpu.VMEM(noise_weights.shape[::-1], jnp.float32),
            pltpu.VMEM((offsets, layers, rows, cells), jnp.bfloat16),
            pltpu.VMEM((offsets + 1, probes, rows), jnp.bfloat16),
            pltpu.VMEM((layers, probes, cells), jnp.float32),
            pltpu.VMEM((chunks, lats - 1, layers, part, band), jnp.bfloat16),
            pltpu.VMEM((chunks, lats - 1, layers, part, band), jnp.bfloat16),
            pltpu.VMEM((layers, probes, band), jnp.float32),
            pltpu.SemaphoreType.DMA((2,)),
            pltpu.SemaphoreType.DMA((offsets,)),
            pltpu.SemaphoreType.DMA((2 * offsets, chunks)),
            pltpu.SemaphoreType.DMA((offsets + 1, chunks)),
            pltpu.SemaphoreType.DMA((chunks, lats - 1)),
            pltpu.SemaphoreType.DMA((chunks, lats - 1)),
        ],
        compiler_params=pltpu.CompilerParams(
            collective_id=0, has_side_effects=True, vmem_limit_bytes=63 * 1024 * 1024
        ),
        cost_estimate=pl.CostEstimate(
            flops=2 * offsets * layers * rows * cells * probes,
            bytes_accessed=2 * offsets * layers * rows * cells,
            transcendentals=0,
        ),
    )(residual, noise_weights.T, kernel)


def solution(mesh):
    return jax.shard_map(
        functools.partial(per_device, mesh.shape["lat"], mesh.shape["lon"]),
        mesh=mesh,
        in_specs=(P("lat", "lon", None), P("lat", "lon"), P(None, None, "lat", None)),
        out_specs=P(None, "lat", "lon", None),
        check_vma=False,
    )
```

```python
import functools

import jax
import jax.numpy as jnp
from jax import lax
from jax.experimental import pallas as pl
from jax.experimental.pallas import tpu as pltpu
from jax.sharding import PartitionSpec as P

MESH = pl.DeviceIdType.MESH


def route(offsets, lons, chunks):
    direct = {d: (-d, 0) for d in range(1, offsets)}
    if lons % 2 or offsets < 3 or lons <= offsets:
        return 1, [[direct] * chunks], list(range(1, offsets))
    transit = offsets
    even, odd = [], []
    for c in range(chunks):
        if c % 2:
            even.append({**direct, 1: (-2, transit), 3: (-4, transit), transit: (1, 0)})
            odd.append({**direct, 3: (-2, 1)})
        else:
            even.append({**direct, 1: (1, 2), 3: (1, transit)})
            odd.append({**direct, 3: (-1, 2), transit: (-4, 0)})
        if offsets == 3:
            for table in (even[c], odd[c]):
                if c % 2 == 0 or table is odd[c]:
                    table.pop(transit, None)
    return 2, [even, odd], [2] + [d for d in range(1, offsets) if d != 2]


def sweep(
    lats, lons, res_hbm, nw_hbm, panel_hbm, out_ref,
    res, nw, panel, blocks, total, outgoing, incoming, summed,
    input_sem, panel_sem, east_send, east_recv, band_send, band_recv,
):
    offsets, layers, rows, cells = panel_hbm.shape
    probes = res_hbm.shape[-1]
    chunks, part = outgoing.shape[0], outgoing.shape[3]
    band = cells // lats
    lat, lon = lax.axis_index("lat"), lax.axis_index("lon")
    period, source, order = route(offsets, lons, chunks)
    pair = 2 if lats % 2 == 0 else 1
    groups = lats // pair

    res_load = pltpu.make_async_copy(res_hbm, res, input_sem.at[0])
    nw_load = pltpu.make_async_copy(nw_hbm, nw, input_sem.at[1])
    res_load.start()
    nw_load.start()
    loads = {}
    for d in [0] + order:
        loads[d] = pltpu.make_async_copy(panel_hbm.at[d], panel.at[d], panel_sem.at[d])
    loads[0].start()

    def along(delta):
        return (lat, lax.rem(lon + (delta + lons), lons))

    def across(a, b):
        to = lax.rem(lat // pair + a, groups) * pair + lax.rem(lat % pair + b, pair)
        return (to, lon)

    partners = [(a, b) for a in range(groups - 1, -1, -1) for b in range(pair)][: lats]
    partners = [ab for ab in partners if ab != (0, 0)]

    sends = [[[] for _ in range(chunks)] for _ in range(period)]
    senders = [set() for _ in range(period)]
    passed = [set() for _ in range(period)]
    for q in range(period):
        for c in range(chunks):
            for d, (delta, held) in sorted(source[q][c].items()):
                by = (q + delta) % period
                sends[by][c].append((-delta, held, d))
                senders[q].add(delta)
                if held > 0:
                    passed[by].add((held, c))

    def urgency(q, c, send):
        delta, _, d = send
        return ((d, c) not in passed[(q + delta) % period], c)

    receivers = [{send[0] for c in range(chunks) for send in sends[q][c]} for q in range(period)]

    def per_parity(action):
        for q in range(period):
            if period == 1:
                action(q)
            else:
                pl.when(lax.rem(lon, period) == q)(functools.partial(action, q))

    barrier = pltpu.get_barrier_semaphore()

    def greet(q):
        for delta in sorted(senders[q]):
            pl.semaphore_signal(barrier, inc=1, device_id=along(delta), device_id_type=MESH)

    per_parity(greet)
    for a, b in partners:
        pl.semaphore_signal(barrier, inc=1, device_id=across(a, b), device_id_type=MESH)

    res_load.wait()
    nw_load.wait()
    columns = res.shape[1]
    pieces = [
        nw[:, y : y + 1] * res[y].astype(jnp.float32) for y in range(rows // columns)
    ]
    blocks[0] = jnp.concatenate(pieces, axis=0).T.astype(jnp.bfloat16)

    def chunk(c):
        return pl.ds(c * part, part)

    def east(q, n, c):
        delta, held, d = sends[q][c][n]
        return pltpu.make_async_remote_copy(
            src_ref=blocks.at[held, chunk(c)],
            dst_ref=blocks.at[d, chunk(c)],
            send_sem=east_send.at[n, c],
            recv_sem=east_recv.at[d, c],
            device_id=along(delta),
            device_id_type=MESH,
        )

    def begin(q):
        first = [
            (urgency(q, c, send), n, c)
            for c in range(chunks)
            for n, send in enumerate(sends[q][c])
            if send[1] == 0
        ]
        for _, n, c in sorted(first):
            east(q, n, c).start()

    def arrive(d, c):
        pltpu.make_async_remote_copy(
            src_ref=blocks.at[d, chunk(c)],
            dst_ref=blocks.at[d, chunk(c)],
            send_sem=east_send.at[0, c],
            recv_sem=east_recv.at[d, c],
            device_id=along(1),
            device_id_type=MESH,
        ).wait_recv()

    def admit(q):
        pl.semaphore_wait(barrier, len(receivers[q]) + len(partners))

    per_parity(admit)
    per_parity(begin)
    for d in order:
        loads[d].start()

    def accumulate(d, first):
        loads[d].wait()
        for l in range(layers):

            @pl.loop(0, lats)
            def _(b):
                cols = pl.ds(pl.multiple_of(b * band, band), band)
                value = jnp.dot(
                    blocks[d], panel[d, l, :, cols], preferred_element_type=jnp.float32
                )
                total[l, :, cols] = value if first else total[l, :, cols] + value

    accumulate(0, True)
    def relay(q):
        for held, c in sorted(passed[q], key=lambda slot: (slot[0] != 2, slot[0])):
            arrive(held, c)
            for n, send in enumerate(sends[q][c]):
                if send[1] == held:
                    east(q, n, c).start()

    def rest(d, c):
        def action(q):
            if (d, c) not in passed[q]:
                arrive(d, c)

        if all((d, c) not in passed[q] for q in range(period)):
            arrive(d, c)
        else:
            per_parity(action)

    per_parity(relay)
    for d in order[:-1]:
        for c in range(chunks):
            rest(d, c)
        accumulate(d, False)

    last = order[-1]
    loads[last].wait()

    def finish(c, to):
        cols = pl.ds(pl.multiple_of(to * band, band), band)
        return [
            total[l, chunk(c), cols]
            + jnp.dot(
                blocks[last, chunk(c)], panel[last, l, :, cols],
                preferred_element_type=jnp.float32,
            )
            for l in range(layers)
        ]

    sent = {}
    for c in range(chunks):
        rest(last, c)
        for n, (a, b) in enumerate(partners):
            to = across(a, b)
            for l, value in enumerate(finish(c, to[0])):
                outgoing[c, n, l] = value.astype(jnp.bfloat16)
            sent[c, n] = pltpu.make_async_remote_copy(
                src_ref=outgoing.at[c, n],
                dst_ref=incoming.at[c, n],
                send_sem=band_send.at[c, n],
                recv_sem=band_recv.at[c, n],
                device_id=to,
                device_id_type=MESH,
            )
            sent[c, n].start()
        for l, value in enumerate(finish(c, lat)):
            summed[l, chunk(c)] = value
    for c in range(chunks):
        for n in reversed(range(len(partners))):
            sent[c, n].wait_recv()
        for l in range(layers):
            value = summed[l, chunk(c)]
            for n in range(len(partners)):
                value = value + incoming[c, n, l].astype(jnp.float32)
            summed[l, chunk(c)] = value
    for l in range(layers):
        out_ref[l] = summed[l].T.reshape(out_ref.shape[1:])

    def drain(q):
        for c in range(chunks):
            for n in range(len(sends[q][c])):
                east(q, n, c).wait_send()

    per_parity(drain)
    for copy in sent.values():
        copy.wait_send()


def per_device(lats, lons, residual, noise_weights, kernel):
    offsets, layers, rows, cells = kernel.shape
    probes = residual.shape[2]
    band = cells // lats
    chunks = 2 if probes % 32 == 0 else 1
    part = probes // chunks
    remote = pl.BlockSpec(memory_space=pltpu.HBM)
    return pl.pallas_call(
        functools.partial(sweep, lats, lons),
        out_shape=jax.ShapeDtypeStruct(
            (layers, residual.shape[0], residual.shape[1], probes), jnp.float32
        ),
        in_specs=[remote, remote, remote],
        out_specs=pl.BlockSpec(memory_space=pltpu.VMEM),
        scratch_shapes=[
            pltpu.VMEM(residual.shape, jnp.bfloat16),
            pltpu.VMEM(noise_weights.shape[::-1], jnp.float32),
            pltpu.VMEM((offsets, layers, rows, cells), jnp.bfloat16),
            pltpu.VMEM((offsets + 1, probes, rows), jnp.bfloat16),
            pltpu.VMEM((layers, probes, cells), jnp.float32),
            pltpu.VMEM((chunks, lats - 1, layers, part, band), jnp.bfloat16),
            pltpu.VMEM((chunks, lats - 1, layers, part, band), jnp.bfloat16),
            pltpu.VMEM((layers, probes, band), jnp.float32),
            pltpu.SemaphoreType.DMA((2,)),
            pltpu.SemaphoreType.DMA((offsets,)),
            pltpu.SemaphoreType.DMA((2 * offsets, chunks)),
            pltpu.SemaphoreType.DMA((offsets + 1, chunks)),
            pltpu.SemaphoreType.DMA((chunks, lats - 1)),
            pltpu.SemaphoreType.DMA((chunks, lats - 1)),
        ],
        compiler_params=pltpu.CompilerParams(
            collective_id=0, has_side_effects=True, vmem_limit_bytes=63 * 1024 * 1024
        ),
        cost_estimate=pl.CostEstimate(
            flops=2 * offsets * layers * rows * cells * probes,
            bytes_accessed=2 * offsets * layers * rows * cells,
            transcendentals=0,
        ),
    )(residual, noise_weights.T, kernel)


def solution(mesh):
    return jax.shard_map(
        functools.partial(per_device, mesh.shape["lat"], mesh.shape["lon"]),
        mesh=mesh,
        in_specs=(P("lat", "lon", None), P("lat", "lon"), P(None, None, "lat", None)),
        out_specs=P(None, "lat", "lon", None),
        check_vma=False,
    )
```

```python
import functools

import jax
import jax.numpy as jnp
from jax import lax
from jax.experimental import pallas as pl
from jax.experimental.pallas import tpu as pltpu
from jax.sharding import PartitionSpec as P

MESH = pl.DeviceIdType.MESH


def route(offsets, lons, chunks):
    direct = {d: (-d, 0) for d in range(1, offsets)}
    if lons % 2 or offsets < 3 or lons <= offsets:
        return 1, [[direct] * chunks], list(range(1, offsets))
    transit = offsets
    even, odd = [], []
    for c in range(chunks):
        if c % 2:
            even.append({**direct, 1: (-2, transit), 3: (-4, transit), transit: (1, 0)})
            odd.append({**direct, 3: (-2, 1)})
        else:
            even.append({**direct, 1: (1, 2), 3: (1, transit)})
            odd.append({**direct, 3: (-1, 2), transit: (-4, 0)})
        if offsets == 3:
            for table in (even[c], odd[c]):
                if c % 2 == 0 or table is odd[c]:
                    table.pop(transit, None)
    return 2, [even, odd], [2] + [d for d in range(1, offsets) if d != 2]


def sweep(
    lats, lons, res_hbm, nw_hbm, panel_hbm, out_ref,
    res, nw, panel, blocks, total, outgoing, incoming,
    input_sem, panel_sem, east_send, east_recv, band_send, band_recv,
):
    offsets, layers, rows, cells = panel_hbm.shape
    probes = res_hbm.shape[-1]
    chunks, part = blocks.shape[1], blocks.shape[2]
    band = cells // lats
    lat, lon = lax.axis_index("lat"), lax.axis_index("lon")
    period, source, order = route(offsets, lons, chunks)
    pair = 2 if lats % 2 == 0 else 1
    groups = lats // pair

    res_load = pltpu.make_async_copy(res_hbm, res, input_sem.at[0])
    nw_load = pltpu.make_async_copy(nw_hbm, nw, input_sem.at[1])
    res_load.start()
    nw_load.start()
    loads = {}
    for d in [0] + order:
        loads[d] = pltpu.make_async_copy(panel_hbm.at[d], panel.at[d], panel_sem.at[d])
    loads[0].start()

    def along(delta):
        return (lat, lax.rem(lon + (delta + lons), lons))

    def across(a, b):
        to = lax.rem(lat // pair + a, groups) * pair + lax.rem(lat % pair + b, pair)
        return (to, lon)

    partners = [(a, b) for a in range(groups - 1, -1, -1) for b in range(pair)][: lats]
    partners = [ab for ab in partners if ab != (0, 0)]

    sends = [[[] for _ in range(chunks)] for _ in range(period)]
    senders = [set() for _ in range(period)]
    passed = [set() for _ in range(period)]
    for q in range(period):
        for c in range(chunks):
            for d, (delta, held) in sorted(source[q][c].items()):
                by = (q + delta) % period
                sends[by][c].append((-delta, held, d))
                senders[q].add(delta)
                if held > 0:
                    passed[by].add((held, c))

    def urgency(q, c, send):
        delta, _, d = send
        return ((d, c) not in passed[(q + delta) % period], c)

    receivers = [{send[0] for c in range(chunks) for send in sends[q][c]} for q in range(period)]

    def per_parity(action):
        for q in range(period):
            if period == 1:
                action(q)
            else:
                pl.when(lax.rem(lon, period) == q)(functools.partial(action, q))

    barrier = pltpu.get_barrier_semaphore()

    def greet(q):
        for delta in sorted(senders[q]):
            pl.semaphore_signal(barrier, inc=1, device_id=along(delta), device_id_type=MESH)

    per_parity(greet)
    for a, b in partners:
        pl.semaphore_signal(barrier, inc=1, device_id=across(a, b), device_id_type=MESH)

    res_load.wait()
    nw_load.wait()
    columns = res.shape[1]
    pieces = [
        nw[:, y : y + 1] * res[y].astype(jnp.float32) for y in range(rows // columns)
    ]
    weighted = jnp.concatenate(pieces, axis=0).astype(jnp.bfloat16)
    blocks[0] = weighted.reshape(chunks, part, probes)

    def east(q, n, c):
        delta, held, d = sends[q][c][n]
        return pltpu.make_async_remote_copy(
            src_ref=blocks.at[held, c],
            dst_ref=blocks.at[d, c],
            send_sem=east_send.at[n, c],
            recv_sem=east_recv.at[d, c],
            device_id=along(delta),
            device_id_type=MESH,
        )

    def begin(q):
        first = [
            (urgency(q, c, send), n, c)
            for c in range(chunks)
            for n, send in enumerate(sends[q][c])
            if send[1] == 0
        ]
        for _, n, c in sorted(first):
            east(q, n, c).start()

    def arrive(d, c):
        pltpu.make_async_remote_copy(
            src_ref=blocks.at[d, c],
            dst_ref=blocks.at[d, c],
            send_sem=east_send.at[0, c],
            recv_sem=east_recv.at[d, c],
            device_id=along(1),
            device_id_type=MESH,
        ).wait_recv()

    def admit(q):
        pl.semaphore_wait(barrier, len(receivers[q]) + len(partners))

    per_parity(admit)
    per_parity(begin)
    for d in order:
        loads[d].start()

    def product(d, l, cols):
        return lax.dot_general(
            panel[d, l, :, cols], blocks[d].reshape(rows, probes),
            (((0,), (0,)), ((), ())), preferred_element_type=jnp.float32,
        )

    def accumulate(d, first):
        loads[d].wait()
        for l in range(layers):
            for b in range(lats):
                cols = pl.ds(b * band, band)
                value = product(d, l, cols)
                total[l, cols] = value if first else total[l, cols] + value

    accumulate(0, True)
    def relay(q):
        for held, c in sorted(passed[q], key=lambda slot: (slot[0] != 2, slot[0])):
            arrive(held, c)
            for n, send in enumerate(sends[q][c]):
                if send[1] == held:
                    east(q, n, c).start()

    def rest(d, c):
        def action(q):
            if (d, c) not in passed[q]:
                arrive(d, c)

        if all((d, c) not in passed[q] for q in range(period)):
            arrive(d, c)
        else:
            per_parity(action)

    per_parity(relay)
    for d in order[:-1]:
        for c in range(chunks):
            rest(d, c)
        accumulate(d, False)

    last = order[-1]
    loads[last].wait()

    for c in range(chunks):
        rest(last, c)

    def finish(to):
        cols = pl.ds(pl.multiple_of(to * band, band), band)
        return [total[l, cols] + product(last, l, cols) for l in range(layers)]

    sent = []
    for n, (a, b) in enumerate(partners):
        to = across(a, b)
        for l, value in enumerate(finish(to[0])):
            outgoing[n, l] = value.astype(jnp.bfloat16)
        copy = pltpu.make_async_remote_copy(
            src_ref=outgoing.at[n],
            dst_ref=incoming.at[n],
            send_sem=band_send.at[n],
            recv_sem=band_recv.at[n],
            device_id=to,
            device_id_type=MESH,
        )
        copy.start()
        sent.append(copy)
    mine = finish(lat)
    for n, copy in reversed(list(enumerate(sent))):
        copy.wait_recv()
        mine = [value + incoming[n, l].astype(jnp.float32) for l, value in enumerate(mine)]
    for l, value in enumerate(mine):
        out_ref[l] = value.reshape(out_ref.shape[1:])

    def drain(q):
        for c in range(chunks):
            for n in range(len(sends[q][c])):
                east(q, n, c).wait_send()

    per_parity(drain)
    for copy in sent:
        copy.wait_send()


def per_device(lats, lons, residual, noise_weights, kernel):
    offsets, layers, rows, cells = kernel.shape
    probes = residual.shape[2]
    band = cells // lats
    chunks = 2 if rows % 32 == 0 else 1
    remote = pl.BlockSpec(memory_space=pltpu.HBM)
    return pl.pallas_call(
        functools.partial(sweep, lats, lons),
        out_shape=jax.ShapeDtypeStruct(
            (layers, residual.shape[0], residual.shape[1], probes), jnp.float32
        ),
        in_specs=[remote, remote, remote],
        out_specs=pl.BlockSpec(memory_space=pltpu.VMEM),
        scratch_shapes=[
            pltpu.VMEM(residual.shape, jnp.bfloat16),
            pltpu.VMEM(noise_weights.shape[::-1], jnp.float32),
            pltpu.VMEM((offsets, layers, rows, cells), jnp.bfloat16),
            pltpu.VMEM((offsets + 1, chunks, rows // chunks, probes), jnp.bfloat16),
            pltpu.VMEM((layers, cells, probes), jnp.float32),
            pltpu.VMEM((lats - 1, layers, band, probes), jnp.bfloat16),
            pltpu.VMEM((lats - 1, layers, band, probes), jnp.bfloat16),
            pltpu.SemaphoreType.DMA((2,)),
            pltpu.SemaphoreType.DMA((offsets,)),
            pltpu.SemaphoreType.DMA((2 * offsets, chunks)),
            pltpu.SemaphoreType.DMA((offsets + 1, chunks)),
            pltpu.SemaphoreType.DMA((lats - 1,)),
            pltpu.SemaphoreType.DMA((lats - 1,)),
        ],
        compiler_params=pltpu.CompilerParams(
            collective_id=0, has_side_effects=True, vmem_limit_bytes=63 * 1024 * 1024
        ),
        cost_estimate=pl.CostEstimate(
            flops=2 * offsets * layers * rows * cells * probes,
            bytes_accessed=2 * offsets * layers * rows * cells,
            transcendentals=0,
        ),
    )(residual, noise_weights.T, kernel)


def solution(mesh):
    return jax.shard_map(
        functools.partial(per_device, mesh.shape["lat"], mesh.shape["lon"]),
        mesh=mesh,
        in_specs=(P("lat", "lon", None), P("lat", "lon"), P(None, None, "lat", None)),
        out_specs=P(None, "lat", "lon", None),
        check_vma=False,
    )
```

```python
import functools

import jax
import jax.numpy as jnp
from jax import lax
from jax.experimental import pallas as pl
from jax.experimental.pallas import tpu as pltpu
from jax.sharding import PartitionSpec as P

MESH = pl.DeviceIdType.MESH


def route(offsets, lons, chunks):
    direct = {d: (-d, 0) for d in range(1, offsets)}
    if lons % 2 or offsets < 3 or lons <= offsets:
        return 1, [[direct] * chunks], list(range(1, offsets))
    transit = offsets
    even, odd = [], []
    for c in range(chunks):
        if c % 2:
            even.append({**direct, 1: (-2, transit), 3: (-4, transit), transit: (1, 0)})
            odd.append({**direct, 3: (-2, 1)})
        else:
            even.append({**direct, 1: (1, 2), 3: (1, transit)})
            odd.append({**direct, 3: (-1, 2), transit: (-4, 0)})
        if offsets == 3:
            for table in (even[c], odd[c]):
                if c % 2 == 0 or table is odd[c]:
                    table.pop(transit, None)
    return 2, [even, odd], [2] + [d for d in range(1, offsets) if d != 2]


def sweep(
    lats, lons, res_hbm, nw_hbm, panel_hbm, out_ref,
    res, nw, panel, blocks, total, outgoing, incoming,
    input_sem, panel_sem, east_send, east_recv, band_send, band_recv,
):
    offsets, layers, rows, cells = panel_hbm.shape
    probes = res_hbm.shape[-1]
    chunks, part = blocks.shape[1], blocks.shape[2]
    band = cells // lats
    lat, lon = lax.axis_index("lat"), lax.axis_index("lon")
    period, source, order = route(offsets, lons, chunks)
    pair = 2 if lats % 2 == 0 else 1
    groups = lats // pair

    res_load = pltpu.make_async_copy(res_hbm, res, input_sem.at[0])
    nw_load = pltpu.make_async_copy(nw_hbm, nw, input_sem.at[1])
    res_load.start()
    nw_load.start()
    loads = {}
    pieces = 8 if rows % 128 == 0 else 1
    for d in [0] + order:
        loads[d] = pltpu.make_async_copy(panel_hbm.at[d], panel.at[d], panel_sem.at[d])
        for n in range(pieces):
            for l in range(layers):
                some = pl.ds(n * (rows // pieces), rows // pieces)
                pltpu.make_async_copy(
                    panel_hbm.at[d, l, some], panel.at[d, l, some], panel_sem.at[d]
                ).start()

    def along(delta):
        return (lat, lax.rem(lon + (delta + lons), lons))

    def across(a, b):
        to = lax.rem(lat // pair + a, groups) * pair + lax.rem(lat % pair + b, pair)
        return (to, lon)

    partners = [(a, b) for a in range(groups - 1, -1, -1) for b in range(pair)][: lats]
    partners = [ab for ab in partners if ab != (0, 0)]

    sends = [[[] for _ in range(chunks)] for _ in range(period)]
    senders = [set() for _ in range(period)]
    passed = [set() for _ in range(period)]
    for q in range(period):
        for c in range(chunks):
            for d, (delta, held) in sorted(source[q][c].items()):
                by = (q + delta) % period
                sends[by][c].append((-delta, held, d))
                senders[q].add(delta)
                if held > 0:
                    passed[by].add((held, c))

    def urgency(q, c, send):
        delta, _, d = send
        return ((d, c) not in passed[(q + delta) % period], c)

    receivers = [{send[0] for c in range(chunks) for send in sends[q][c]} for q in range(period)]

    def per_parity(action):
        for q in range(period):
            if period == 1:
                action(q)
            else:
                pl.when(lax.rem(lon, period) == q)(functools.partial(action, q))

    barrier = pltpu.get_barrier_semaphore()

    def greet(q):
        for delta in sorted(senders[q]):
            pl.semaphore_signal(barrier, inc=1, device_id=along(delta), device_id_type=MESH)

    per_parity(greet)
    for a, b in partners:
        pl.semaphore_signal(barrier, inc=1, device_id=across(a, b), device_id_type=MESH)

    res_load.wait()
    nw_load.wait()
    columns = res.shape[1]
    pieces = [
        nw[:, y : y + 1] * res[y].astype(jnp.float32) for y in range(rows // columns)
    ]
    weighted = jnp.concatenate(pieces, axis=0).astype(jnp.bfloat16)
    blocks[0] = weighted.reshape(chunks, part, probes)

    def east(q, n, c):
        delta, held, d = sends[q][c][n]
        return pltpu.make_async_remote_copy(
            src_ref=blocks.at[held, c],
            dst_ref=blocks.at[d, c],
            send_sem=east_send.at[n, c],
            recv_sem=east_recv.at[d, c],
            device_id=along(delta),
            device_id_type=MESH,
        )

    def begin(q):
        first = [
            (urgency(q, c, send), n, c)
            for c in range(chunks)
            for n, send in enumerate(sends[q][c])
            if send[1] == 0
        ]
        for _, n, c in sorted(first):
            east(q, n, c).start()

    def arrive(d, c):
        pltpu.make_async_remote_copy(
            src_ref=blocks.at[d, c],
            dst_ref=blocks.at[d, c],
            send_sem=east_send.at[0, c],
            recv_sem=east_recv.at[d, c],
            device_id=along(1),
            device_id_type=MESH,
        ).wait_recv()

    def admit(q):
        pl.semaphore_wait(barrier, len(receivers[q]) + len(partners))

    per_parity(admit)
    per_parity(begin)

    def product(d, l, cols):
        return lax.dot_general(
            panel[d, l, :, cols], blocks[d].reshape(rows, probes),
            (((0,), (0,)), ((), ())), preferred_element_type=jnp.float32,
        )

    def accumulate(d, first):
        loads[d].wait()
        for l in range(layers):
            for b in range(lats):
                cols = pl.ds(b * band, band)
                value = product(d, l, cols)
                total[l, cols] = value if first else total[l, cols] + value

    accumulate(0, True)
    def relay(q):
        for held, c in sorted(passed[q], key=lambda slot: (slot[0] != 2, slot[0])):
            arrive(held, c)
            for n, send in enumerate(sends[q][c]):
                if send[1] == held:
                    east(q, n, c).start()

    def rest(d, c):
        def action(q):
            if (d, c) not in passed[q]:
                arrive(d, c)

        if all((d, c) not in passed[q] for q in range(period)):
            arrive(d, c)
        else:
            per_parity(action)

    per_parity(relay)
    for d in order[:-1]:
        for c in range(chunks):
            rest(d, c)
        accumulate(d, False)

    last = order[-1]
    loads[last].wait()

    for c in range(chunks):
        rest(last, c)

    def finish(to):
        cols = pl.ds(pl.multiple_of(to * band, band), band)
        return [total[l, cols] + product(last, l, cols) for l in range(layers)]

    sent = []
    for n, (a, b) in enumerate(partners):
        to = across(a, b)
        for l, value in enumerate(finish(to[0])):
            outgoing[n, l] = value.astype(jnp.bfloat16)
        copy = pltpu.make_async_remote_copy(
            src_ref=outgoing.at[n],
            dst_ref=incoming.at[n],
            send_sem=band_send.at[n],
            recv_sem=band_recv.at[n],
            device_id=to,
            device_id_type=MESH,
        )
        copy.start()
        sent.append(copy)
    mine = finish(lat)
    for n, copy in reversed(list(enumerate(sent))):
        copy.wait_recv()
        mine = [value + incoming[n, l].astype(jnp.float32) for l, value in enumerate(mine)]
    for l, value in enumerate(mine):
        out_ref[l] = value.reshape(out_ref.shape[1:])

    def drain(q):
        for c in range(chunks):
            for n in range(len(sends[q][c])):
                east(q, n, c).wait_send()

    per_parity(drain)
    for copy in sent:
        copy.wait_send()


def per_device(lats, lons, residual, noise_weights, kernel):
    offsets, layers, rows, cells = kernel.shape
    probes = residual.shape[2]
    band = cells // lats
    chunks = 2 if rows % 32 == 0 else 1
    remote = pl.BlockSpec(memory_space=pltpu.HBM)
    return pl.pallas_call(
        functools.partial(sweep, lats, lons),
        out_shape=jax.ShapeDtypeStruct(
            (layers, residual.shape[0], residual.shape[1], probes), jnp.float32
        ),
        in_specs=[remote, remote, remote],
        out_specs=pl.BlockSpec(memory_space=pltpu.VMEM),
        scratch_shapes=[
            pltpu.VMEM(residual.shape, jnp.bfloat16),
            pltpu.VMEM(noise_weights.shape[::-1], jnp.float32),
            pltpu.VMEM((offsets, layers, rows, cells), jnp.bfloat16),
            pltpu.VMEM((offsets + 1, chunks, rows // chunks, probes), jnp.bfloat16),
            pltpu.VMEM((layers, cells, probes), jnp.float32),
            pltpu.VMEM((lats - 1, layers, band, probes), jnp.bfloat16),
            pltpu.VMEM((lats - 1, layers, band, probes), jnp.bfloat16),
            pltpu.SemaphoreType.DMA((2,)),
            pltpu.SemaphoreType.DMA((offsets,)),
            pltpu.SemaphoreType.DMA((2 * offsets, chunks)),
            pltpu.SemaphoreType.DMA((offsets + 1, chunks)),
            pltpu.SemaphoreType.DMA((lats - 1,)),
            pltpu.SemaphoreType.DMA((lats - 1,)),
        ],
        compiler_params=pltpu.CompilerParams(
            collective_id=0, has_side_effects=True, vmem_limit_bytes=63 * 1024 * 1024
        ),
        cost_estimate=pl.CostEstimate(
            flops=2 * offsets * layers * rows * cells * probes,
            bytes_accessed=2 * offsets * layers * rows * cells,
            transcendentals=0,
        ),
    )(residual, noise_weights.T, kernel)


def solution(mesh):
    return jax.shard_map(
        functools.partial(per_device, mesh.shape["lat"], mesh.shape["lon"]),
        mesh=mesh,
        in_specs=(P("lat", "lon", None), P("lat", "lon"), P(None, None, "lat", None)),
        out_specs=P(None, "lat", "lon", None),
        check_vma=False,
    )
```

```python
import functools

import jax
import jax.numpy as jnp
from jax import lax
from jax.experimental import pallas as pl
from jax.experimental.pallas import tpu as pltpu
from jax.sharding import PartitionSpec as P

MESH = pl.DeviceIdType.MESH


def route(offsets, lons, chunks):
    direct = {d: (-d, 0) for d in range(1, offsets)}
    if lons % 2 or offsets < 3 or lons <= offsets:
        return 1, [[direct] * chunks], list(range(1, offsets))
    transit = offsets
    even, odd = [], []
    for c in range(chunks):
        if c % 2:
            even.append({**direct, 1: (-2, transit), 3: (-4, transit), transit: (1, 0)})
            odd.append({**direct, 3: (-2, 1)})
        else:
            even.append({**direct, 1: (1, 2), 3: (1, transit)})
            odd.append({**direct, 3: (-1, 2), transit: (-4, 0)})
        if offsets == 3:
            for table in (even[c], odd[c]):
                if c % 2 == 0 or table is odd[c]:
                    table.pop(transit, None)
    return 2, [even, odd], [2] + [d for d in range(1, offsets) if d != 2]


def sweep(
    lats, lons, res_hbm, nw_hbm, panel_hbm, out_ref,
    res, nw, panel, blocks, total, outgoing, incoming,
    input_sem, panel_sem, east_send, east_recv, band_send, band_recv,
):
    offsets, layers, rows, cells = panel_hbm.shape
    probes = res_hbm.shape[-1]
    chunks, part = blocks.shape[1], blocks.shape[2]
    band = cells // lats
    lat, lon = lax.axis_index("lat"), lax.axis_index("lon")
    period, source, order = route(offsets, lons, chunks)
    pair = 2 if lats % 2 == 0 else 1
    groups = lats // pair

    res_load = pltpu.make_async_copy(res_hbm, res, input_sem.at[0])
    nw_load = pltpu.make_async_copy(nw_hbm, nw, input_sem.at[1])
    res_load.start()
    nw_load.start()
    loads = {}
    for d in [0] + order:
        loads[d] = pltpu.make_async_copy(panel_hbm.at[d], panel.at[d], panel_sem.at[d])
    loads[0].start()

    def along(delta):
        return (lat, lax.rem(lon + (delta + lons), lons))

    def across(a, b):
        to = lax.rem(lat // pair + a, groups) * pair + lax.rem(lat % pair + b, pair)
        return (to, lon)

    partners = [(a, b) for a in range(groups - 1, -1, -1) for b in range(pair)][: lats]
    partners = [ab for ab in partners if ab != (0, 0)]

    sends = [[[] for _ in range(chunks)] for _ in range(period)]
    senders = [set() for _ in range(period)]
    passed = [set() for _ in range(period)]
    for q in range(period):
        for c in range(chunks):
            for d, (delta, held) in sorted(source[q][c].items()):
                by = (q + delta) % period
                sends[by][c].append((-delta, held, d))
                senders[q].add(delta)
                if held > 0:
                    passed[by].add((held, c))

    def urgency(q, c, send):
        delta, _, d = send
        return ((d, c) not in passed[(q + delta) % period], c)

    receivers = [{send[0] for c in range(chunks) for send in sends[q][c]} for q in range(period)]

    def per_parity(action):
        for q in range(period):
            if period == 1:
                action(q)
            else:
                pl.when(lax.rem(lon, period) == q)(functools.partial(action, q))

    barrier = pltpu.get_barrier_semaphore()

    def greet(q):
        for delta in sorted(senders[q]):
            pl.semaphore_signal(barrier, inc=1, device_id=along(delta), device_id_type=MESH)

    per_parity(greet)
    for a, b in partners:
        pl.semaphore_signal(barrier, inc=1, device_id=across(a, b), device_id_type=MESH)

    res_load.wait()
    nw_load.wait()
    columns = res.shape[1]
    pieces = [
        nw[:, y : y + 1] * res[y].astype(jnp.float32) for y in range(rows // columns)
    ]
    weighted = jnp.concatenate(pieces, axis=0).astype(jnp.bfloat16)
    blocks[0] = weighted.reshape(chunks, part, probes)

    def east(q, n, c):
        delta, held, d = sends[q][c][n]
        return pltpu.make_async_remote_copy(
            src_ref=blocks.at[held, c],
            dst_ref=blocks.at[d, c],
            send_sem=east_send.at[n, c],
            recv_sem=east_recv.at[d, c],
            device_id=along(delta),
            device_id_type=MESH,
        )

    def begin(q):
        first = [
            (urgency(q, c, send), n, c)
            for c in range(chunks)
            for n, send in enumerate(sends[q][c])
            if send[1] == 0
        ]
        for _, n, c in sorted(first):
            east(q, n, c).start()

    def arrive(d, c):
        pltpu.make_async_remote_copy(
            src_ref=blocks.at[d, c],
            dst_ref=blocks.at[d, c],
            send_sem=east_send.at[0, c],
            recv_sem=east_recv.at[d, c],
            device_id=along(1),
            device_id_type=MESH,
        ).wait_recv()

    def admit(q):
        pl.semaphore_wait(barrier, len(receivers[q]) + len(partners))

    per_parity(admit)
    per_parity(begin)
    loads[order[0]].start()

    def product(d, l, cols):
        return lax.dot_general(
            panel[d, l, :, cols], blocks[d].reshape(rows, probes),
            (((0,), (0,)), ((), ())), preferred_element_type=jnp.float32,
        )

    def accumulate(d, first):
        loads[d].wait()
        for l in range(layers):
            for b in range(lats):
                cols = pl.ds(b * band, band)
                value = product(d, l, cols)
                total[l, cols] = value if first else total[l, cols] + value

    accumulate(0, True)
    def relay(q):
        for held, c in sorted(passed[q], key=lambda slot: (slot[0] != 2, slot[0])):
            arrive(held, c)
            for n, send in enumerate(sends[q][c]):
                if send[1] == held:
                    east(q, n, c).start()

    def rest(d, c):
        def action(q):
            if (d, c) not in passed[q]:
                arrive(d, c)

        if all((d, c) not in passed[q] for q in range(period)):
            arrive(d, c)
        else:
            per_parity(action)

    per_parity(relay)
    for d in order[1:]:
        loads[d].start()
    for d in order[:-1]:
        for c in range(chunks):
            rest(d, c)
        accumulate(d, False)

    last = order[-1]
    loads[last].wait()

    for c in range(chunks):
        rest(last, c)

    def finish(to):
        cols = pl.ds(pl.multiple_of(to * band, band), band)
        return [total[l, cols] + product(last, l, cols) for l in range(layers)]

    sent = []
    for n, (a, b) in enumerate(partners):
        to = across(a, b)
        for l, value in enumerate(finish(to[0])):
            outgoing[n, l] = value.astype(jnp.bfloat16)
        copy = pltpu.make_async_remote_copy(
            src_ref=outgoing.at[n],
            dst_ref=incoming.at[n],
            send_sem=band_send.at[n],
            recv_sem=band_recv.at[n],
            device_id=to,
            device_id_type=MESH,
        )
        copy.start()
        sent.append(copy)
    mine = finish(lat)
    for n, copy in reversed(list(enumerate(sent))):
        copy.wait_recv()
        mine = [value + incoming[n, l].astype(jnp.float32) for l, value in enumerate(mine)]
    for l, value in enumerate(mine):
        out_ref[l] = value.reshape(out_ref.shape[1:])

    def drain(q):
        for c in range(chunks):
            for n in range(len(sends[q][c])):
                east(q, n, c).wait_send()

    per_parity(drain)
    for copy in sent:
        copy.wait_send()


def per_device(lats, lons, residual, noise_weights, kernel):
    offsets, layers, rows, cells = kernel.shape
    probes = residual.shape[2]
    band = cells // lats
    chunks = 2 if rows % 32 == 0 else 1
    remote = pl.BlockSpec(memory_space=pltpu.HBM)
    return pl.pallas_call(
        functools.partial(sweep, lats, lons),
        out_shape=jax.ShapeDtypeStruct(
            (layers, residual.shape[0], residual.shape[1], probes), jnp.float32
        ),
        in_specs=[remote, remote, remote],
        out_specs=pl.BlockSpec(memory_space=pltpu.VMEM),
        scratch_shapes=[
            pltpu.VMEM(residual.shape, jnp.bfloat16),
            pltpu.VMEM(noise_weights.shape[::-1], jnp.float32),
            pltpu.VMEM((offsets, layers, rows, cells), jnp.bfloat16),
            pltpu.VMEM((offsets + 1, chunks, rows // chunks, probes), jnp.bfloat16),
            pltpu.VMEM((layers, cells, probes), jnp.float32),
            pltpu.VMEM((lats - 1, layers, band, probes), jnp.bfloat16),
            pltpu.VMEM((lats - 1, layers, band, probes), jnp.bfloat16),
            pltpu.SemaphoreType.DMA((2,)),
            pltpu.SemaphoreType.DMA((offsets,)),
            pltpu.SemaphoreType.DMA((2 * offsets, chunks)),
            pltpu.SemaphoreType.DMA((offsets + 1, chunks)),
            pltpu.SemaphoreType.DMA((lats - 1,)),
            pltpu.SemaphoreType.DMA((lats - 1,)),
        ],
        compiler_params=pltpu.CompilerParams(
            collective_id=0, has_side_effects=True, vmem_limit_bytes=63 * 1024 * 1024
        ),
        cost_estimate=pl.CostEstimate(
            flops=2 * offsets * layers * rows * cells * probes,
            bytes_accessed=2 * offsets * layers * rows * cells,
            transcendentals=0,
        ),
    )(residual, noise_weights.T, kernel)


def solution(mesh):
    return jax.shard_map(
        functools.partial(per_device, mesh.shape["lat"], mesh.shape["lon"]),
        mesh=mesh,
        in_specs=(P("lat", "lon", None), P("lat", "lon"), P(None, None, "lat", None)),
        out_specs=P(None, "lat", "lon", None),
        check_vma=False,
    )
```

```python
import functools

import jax
import jax.numpy as jnp
from jax import lax
from jax.experimental import pallas as pl
from jax.experimental.pallas import tpu as pltpu
from jax.sharding import PartitionSpec as P

MESH = pl.DeviceIdType.MESH


def route(offsets, lons, chunks):
    direct = {d: (-d, 0) for d in range(1, offsets)}
    if lons % 2 or offsets < 3 or lons <= offsets:
        return 1, [[direct] * chunks], list(range(1, offsets))
    transit = offsets
    even, odd = [], []
    for c in range(chunks):
        if c % 2:
            even.append({**direct, 1: (-2, transit), 3: (-4, transit), transit: (1, 0)})
            odd.append({**direct, 3: (-2, 1)})
        else:
            even.append({**direct, 1: (1, 2), 3: (1, transit)})
            odd.append({**direct, 3: (-1, 2), transit: (-4, 0)})
        if offsets == 3:
            for table in (even[c], odd[c]):
                if c % 2 == 0 or table is odd[c]:
                    table.pop(transit, None)
    return 2, [even, odd], [2] + [d for d in range(1, offsets) if d != 2]


def sweep(
    lats, lons, res_hbm, nw_hbm, panel_hbm, out_ref,
    res, nw, panel, blocks, total, chip_out, chip_in, band_out, band_in,
    input_sem, panel_sem, east_send, east_recv, chip_send, chip_recv, band_send, band_recv,
):
    offsets, layers, rows, cells = panel_hbm.shape
    probes = res_hbm.shape[-1]
    chunks, part = blocks.shape[1], blocks.shape[2]
    band = cells // lats
    lat, lon = lax.axis_index("lat"), lax.axis_index("lon")
    period, source, order = route(offsets, lons, chunks)
    pair = 2 if lats % 2 == 0 else 1
    groups = lats // pair

    res_load = pltpu.make_async_copy(res_hbm, res, input_sem.at[0])
    nw_load = pltpu.make_async_copy(nw_hbm, nw, input_sem.at[1])
    res_load.start()
    nw_load.start()
    loads = {}
    for d in [0] + order:
        loads[d] = pltpu.make_async_copy(panel_hbm.at[d], panel.at[d], panel_sem.at[d])
    loads[0].start()

    def along(delta):
        return (lat, lax.rem(lon + (delta + lons), lons))

    def across(a, b):
        to = lax.rem(lat // pair + a, groups) * pair + lax.rem(lat % pair + b, pair)
        return (to, lon)

    partners = [(a, 0) for a in range(1, groups)] + [(0, b) for b in range(1, pair)]

    sends = [[[] for _ in range(chunks)] for _ in range(period)]
    senders = [set() for _ in range(period)]
    passed = [set() for _ in range(period)]
    for q in range(period):
        for c in range(chunks):
            for d, (delta, held) in sorted(source[q][c].items()):
                by = (q + delta) % period
                sends[by][c].append((-delta, held, d))
                senders[q].add(delta)
                if held > 0:
                    passed[by].add((held, c))

    def urgency(q, c, send):
        delta, _, d = send
        return ((d, c) not in passed[(q + delta) % period], c)

    receivers = [{send[0] for c in range(chunks) for send in sends[q][c]} for q in range(period)]

    def per_parity(action):
        for q in range(period):
            if period == 1:
                action(q)
            else:
                pl.when(lax.rem(lon, period) == q)(functools.partial(action, q))

    barrier = pltpu.get_barrier_semaphore()

    def greet(q):
        for delta in sorted(senders[q]):
            pl.semaphore_signal(barrier, inc=1, device_id=along(delta), device_id_type=MESH)

    per_parity(greet)
    for a, b in partners:
        pl.semaphore_signal(barrier, inc=1, device_id=across(a, b), device_id_type=MESH)

    res_load.wait()
    nw_load.wait()
    columns = res.shape[1]
    pieces = [
        nw[:, y : y + 1] * res[y].astype(jnp.float32) for y in range(rows // columns)
    ]
    weighted = jnp.concatenate(pieces, axis=0).astype(jnp.bfloat16)
    blocks[0] = weighted.reshape(chunks, part, probes)

    def east(q, n, c):
        delta, held, d = sends[q][c][n]
        return pltpu.make_async_remote_copy(
            src_ref=blocks.at[held, c],
            dst_ref=blocks.at[d, c],
            send_sem=east_send.at[n, c],
            recv_sem=east_recv.at[d, c],
            device_id=along(delta),
            device_id_type=MESH,
        )

    def begin(q):
        first = [
            (urgency(q, c, send), n, c)
            for c in range(chunks)
            for n, send in enumerate(sends[q][c])
            if send[1] == 0
        ]
        for _, n, c in sorted(first):
            east(q, n, c).start()

    def arrive(d, c):
        pltpu.make_async_remote_copy(
            src_ref=blocks.at[d, c],
            dst_ref=blocks.at[d, c],
            send_sem=east_send.at[0, c],
            recv_sem=east_recv.at[d, c],
            device_id=along(1),
            device_id_type=MESH,
        ).wait_recv()

    def admit(q):
        pl.semaphore_wait(barrier, len(receivers[q]) + len(partners))

    per_parity(admit)
    per_parity(begin)
    loads[order[0]].start()

    def product(d, l, cols):
        return lax.dot_general(
            panel[d, l, :, cols], blocks[d].reshape(rows, probes),
            (((0,), (0,)), ((), ())), preferred_element_type=jnp.float32,
        )

    def accumulate(d, first):
        loads[d].wait()
        for l in range(layers):
            for b in range(lats):
                cols = pl.ds(b * band, band)
                value = product(d, l, cols)
                total[l, cols] = value if first else total[l, cols] + value

    accumulate(0, True)
    def relay(q):
        for held, c in sorted(passed[q], key=lambda slot: (slot[0] != 2, slot[0])):
            arrive(held, c)
            for n, send in enumerate(sends[q][c]):
                if send[1] == held:
                    east(q, n, c).start()

    def rest(d, c):
        def action(q):
            if (d, c) not in passed[q]:
                arrive(d, c)

        if all((d, c) not in passed[q] for q in range(period)):
            arrive(d, c)
        else:
            per_parity(action)

    per_parity(relay)
    for d in order[1:]:
        loads[d].start()
    for d in order[:-1]:
        for c in range(chunks):
            rest(d, c)
        accumulate(d, False)

    last = order[-1]
    loads[last].wait()

    for c in range(chunks):
        rest(last, c)

    def finish(to):
        cols = pl.ds(pl.multiple_of(to * band, band), band)
        return [total[l, cols] + product(last, l, cols) for l in range(layers)]

    def inner(a, b):
        return pltpu.make_async_remote_copy(
            src_ref=chip_out.at[a, b - 1],
            dst_ref=chip_in.at[a, b - 1],
            send_sem=chip_send.at[a, b - 1],
            recv_sem=chip_recv.at[a, b - 1],
            device_id=across(0, b),
            device_id_type=MESH,
        )

    def outer(a):
        return pltpu.make_async_remote_copy(
            src_ref=band_out.at[a - 1],
            dst_ref=band_in.at[a - 1],
            send_sem=band_send.at[a - 1],
            recv_sem=band_recv.at[a - 1],
            device_id=across(a, 0),
            device_id_type=MESH,
        )

    def offer(a):
        for b in range(1, pair):
            for l, value in enumerate(finish(across(a, b)[0])):
                chip_out[a, b - 1, l] = value.astype(jnp.bfloat16)
            inner(a, b).start()

    def collect(a, values):
        for b in range(1, pair):
            inner(a, b).wait_recv()
            values = [
                value + chip_in[a, b - 1, l].astype(jnp.float32)
                for l, value in enumerate(values)
            ]
        return values

    steps = list(range(1, groups)) + [0]
    offer(steps[0])
    for n, a in enumerate(steps):
        mine = finish(across(a, 0)[0])
        if n + 1 < groups:
            offer(steps[n + 1])
        mine = collect(a, mine)
        if a > 0:
            for l, value in enumerate(mine):
                band_out[a - 1, l] = value.astype(jnp.bfloat16)
            outer(a).start()
    for a in range(1, groups):
        outer(a).wait_recv()
        mine = [
            value + band_in[a - 1, l].astype(jnp.float32) for l, value in enumerate(mine)
        ]
    for l, value in enumerate(mine):
        out_ref[l] = value.reshape(out_ref.shape[1:])

    def drain(q):
        for c in range(chunks):
            for n in range(len(sends[q][c])):
                east(q, n, c).wait_send()

    per_parity(drain)
    for a in range(groups):
        for b in range(1, pair):
            inner(a, b).wait_send()
        if a > 0:
            outer(a).wait_send()


def per_device(lats, lons, residual, noise_weights, kernel):
    offsets, layers, rows, cells = kernel.shape
    probes = residual.shape[2]
    band = cells // lats
    chunks = 2 if rows % 32 == 0 else 1
    pair = 2 if lats % 2 == 0 else 1
    groups = lats // pair
    inner, outer = max(pair - 1, 1), max(groups - 1, 1)
    remote = pl.BlockSpec(memory_space=pltpu.HBM)
    return pl.pallas_call(
        functools.partial(sweep, lats, lons),
        out_shape=jax.ShapeDtypeStruct(
            (layers, residual.shape[0], residual.shape[1], probes), jnp.float32
        ),
        in_specs=[remote, remote, remote],
        out_specs=pl.BlockSpec(memory_space=pltpu.VMEM),
        scratch_shapes=[
            pltpu.VMEM(residual.shape, jnp.bfloat16),
            pltpu.VMEM(noise_weights.shape[::-1], jnp.float32),
            pltpu.VMEM((offsets, layers, rows, cells), jnp.bfloat16),
            pltpu.VMEM((offsets + 1, chunks, rows // chunks, probes), jnp.bfloat16),
            pltpu.VMEM((layers, cells, probes), jnp.float32),
            pltpu.VMEM((groups, inner, layers, band, probes), jnp.bfloat16),
            pltpu.VMEM((groups, inner, layers, band, probes), jnp.bfloat16),
            pltpu.VMEM((outer, layers, band, probes), jnp.bfloat16),
            pltpu.VMEM((outer, layers, band, probes), jnp.bfloat16),
            pltpu.SemaphoreType.DMA((2,)),
            pltpu.SemaphoreType.DMA((offsets,)),
            pltpu.SemaphoreType.DMA((2 * offsets, chunks)),
            pltpu.SemaphoreType.DMA((offsets + 1, chunks)),
            pltpu.SemaphoreType.DMA((groups, inner)),
            pltpu.SemaphoreType.DMA((groups, inner)),
            pltpu.SemaphoreType.DMA((outer,)),
            pltpu.SemaphoreType.DMA((outer,)),
        ],
        compiler_params=pltpu.CompilerParams(
            collective_id=0, has_side_effects=True, vmem_limit_bytes=63 * 1024 * 1024
        ),
        cost_estimate=pl.CostEstimate(
            flops=2 * offsets * layers * rows * cells * probes,
            bytes_accessed=2 * offsets * layers * rows * cells,
            transcendentals=0,
        ),
    )(residual, noise_weights.T, kernel)


def solution(mesh):
    return jax.shard_map(
        functools.partial(per_device, mesh.shape["lat"], mesh.shape["lon"]),
        mesh=mesh,
        in_specs=(P("lat", "lon", None), P("lat", "lon"), P(None, None, "lat", None)),
        out_specs=P(None, "lat", "lon", None),
        check_vma=False,
    )
```

```python
import functools

import jax
import jax.numpy as jnp
from jax import lax
from jax.experimental import pallas as pl
from jax.experimental.pallas import tpu as pltpu
from jax.sharding import PartitionSpec as P

MESH = pl.DeviceIdType.MESH


def route(offsets, lons, chunks):
    direct = {d: (-d, 0) for d in range(1, offsets)}
    if lons % 2 or offsets < 3 or lons <= offsets:
        return 1, [[direct] * chunks], list(range(1, offsets))
    transit = offsets
    even, odd = [], []
    for c in range(chunks):
        if c % 2:
            even.append({**direct, 1: (-2, transit), 3: (-4, transit), transit: (1, 0)})
            odd.append({**direct, 3: (-2, 1)})
        else:
            even.append({**direct, 1: (1, 2), 3: (1, transit)})
            odd.append({**direct, 3: (-1, 2), transit: (-4, 0)})
        if offsets == 3:
            for table in (even[c], odd[c]):
                if c % 2 == 0 or table is odd[c]:
                    table.pop(transit, None)
    return 2, [even, odd], [2] + [d for d in range(1, offsets) if d != 2]


def sweep(
    lats, lons, res_hbm, nw_hbm, panel_hbm, out_ref,
    res, nw, panel, blocks, total, outgoing, incoming,
    input_sem, panel_sem, east_send, east_recv, band_send, band_recv,
):
    offsets, layers, rows, cells = panel_hbm.shape
    probes = res_hbm.shape[-1]
    chunks, part = blocks.shape[1], blocks.shape[2]
    band = cells // lats
    lat, lon = lax.axis_index("lat"), lax.axis_index("lon")
    period, source, order = route(offsets, lons, chunks)
    pair = 2 if lats % 2 == 0 else 1
    groups = lats // pair

    res_load = pltpu.make_async_copy(res_hbm, res, input_sem.at[0])
    nw_load = pltpu.make_async_copy(nw_hbm, nw, input_sem.at[1])
    res_load.start()
    nw_load.start()
    loads = {}
    for d in [0] + order:
        loads[d] = pltpu.make_async_copy(panel_hbm.at[d], panel.at[d], panel_sem.at[d])

    def along(delta):
        return (lat, lax.rem(lon + (delta + lons), lons))

    def across(a, b):
        to = lax.rem(lat // pair + a, groups) * pair + lax.rem(lat % pair + b, pair)
        return (to, lon)

    partners = [(a, b) for a in range(groups - 1, -1, -1) for b in range(pair)][: lats]
    partners = [ab for ab in partners if ab != (0, 0)]

    sends = [[[] for _ in range(chunks)] for _ in range(period)]
    senders = [set() for _ in range(period)]
    passed = [set() for _ in range(period)]
    for q in range(period):
        for c in range(chunks):
            for d, (delta, held) in sorted(source[q][c].items()):
                by = (q + delta) % period
                sends[by][c].append((-delta, held, d))
                senders[q].add(delta)
                if held > 0:
                    passed[by].add((held, c))

    def urgency(q, c, send):
        delta, _, d = send
        return ((d, c) not in passed[(q + delta) % period], c)

    receivers = [{send[0] for c in range(chunks) for send in sends[q][c]} for q in range(period)]

    def per_parity(action):
        for q in range(period):
            if period == 1:
                action(q)
            else:
                pl.when(lax.rem(lon, period) == q)(functools.partial(action, q))

    barrier = pltpu.get_barrier_semaphore()

    def greet(q):
        for delta in sorted(senders[q]):
            pl.semaphore_signal(barrier, inc=1, device_id=along(delta), device_id_type=MESH)

    per_parity(greet)
    for a, b in partners:
        pl.semaphore_signal(barrier, inc=1, device_id=across(a, b), device_id_type=MESH)

    res_load.wait()
    nw_load.wait()
    columns = res.shape[1]
    pieces = [
        nw[:, y : y + 1] * res[y].astype(jnp.float32) for y in range(rows // columns)
    ]
    weighted = jnp.concatenate(pieces, axis=0).astype(jnp.bfloat16)
    blocks[0] = weighted.reshape(chunks, part, probes)

    def east(q, n, c):
        delta, held, d = sends[q][c][n]
        return pltpu.make_async_remote_copy(
            src_ref=blocks.at[held, c],
            dst_ref=blocks.at[d, c],
            send_sem=east_send.at[n, c],
            recv_sem=east_recv.at[d, c],
            device_id=along(delta),
            device_id_type=MESH,
        )

    def begin(q):
        first = [
            (urgency(q, c, send), n, c)
            for c in range(chunks)
            for n, send in enumerate(sends[q][c])
            if send[1] == 0
        ]
        for _, n, c in sorted(first):
            east(q, n, c).start()

    def arrive(d, c):
        pltpu.make_async_remote_copy(
            src_ref=blocks.at[d, c],
            dst_ref=blocks.at[d, c],
            send_sem=east_send.at[0, c],
            recv_sem=east_recv.at[d, c],
            device_id=along(1),
            device_id_type=MESH,
        ).wait_recv()

    def admit(q):
        pl.semaphore_wait(barrier, len(receivers[q]) + len(partners))

    per_parity(admit)
    per_parity(begin)
    loads[0].start()
    loads[order[0]].start()

    def product(d, l, cols):
        return lax.dot_general(
            panel[d, l, :, cols], blocks[d].reshape(rows, probes),
            (((0,), (0,)), ((), ())), preferred_element_type=jnp.float32,
        )

    def accumulate(d, first):
        loads[d].wait()
        for l in range(layers):
            for b in range(lats):
                cols = pl.ds(b * band, band)
                value = product(d, l, cols)
                total[l, cols] = value if first else total[l, cols] + value

    accumulate(0, True)
    def relay(q):
        for held, c in sorted(passed[q], key=lambda slot: (slot[0] != 2, slot[0])):
            arrive(held, c)
            for n, send in enumerate(sends[q][c]):
                if send[1] == held:
                    east(q, n, c).start()

    def rest(d, c):
        def action(q):
            if (d, c) not in passed[q]:
                arrive(d, c)

        if all((d, c) not in passed[q] for q in range(period)):
            arrive(d, c)
        else:
            per_parity(action)

    per_parity(relay)
    for d in order[1:]:
        loads[d].start()
    for d in order[:-1]:
        for c in range(chunks):
            rest(d, c)
        accumulate(d, False)

    last = order[-1]
    loads[last].wait()

    for c in range(chunks):
        rest(last, c)

    def finish(to):
        cols = pl.ds(pl.multiple_of(to * band, band), band)
        return [total[l, cols] + product(last, l, cols) for l in range(layers)]

    sent = []
    for n, (a, b) in enumerate(partners):
        to = across(a, b)
        for l, value in enumerate(finish(to[0])):
            outgoing[n, l] = value.astype(jnp.bfloat16)
        copy = pltpu.make_async_remote_copy(
            src_ref=outgoing.at[n],
            dst_ref=incoming.at[n],
            send_sem=band_send.at[n],
            recv_sem=band_recv.at[n],
            device_id=to,
            device_id_type=MESH,
        )
        copy.start()
        sent.append(copy)
    mine = finish(lat)
    for n, copy in reversed(list(enumerate(sent))):
        copy.wait_recv()
        mine = [value + incoming[n, l].astype(jnp.float32) for l, value in enumerate(mine)]
    for l, value in enumerate(mine):
        out_ref[l] = value.reshape(out_ref.shape[1:])

    def drain(q):
        for c in range(chunks):
            for n in range(len(sends[q][c])):
                east(q, n, c).wait_send()

    per_parity(drain)
    for copy in sent:
        copy.wait_send()


def per_device(lats, lons, residual, noise_weights, kernel):
    offsets, layers, rows, cells = kernel.shape
    probes = residual.shape[2]
    band = cells // lats
    chunks = 2 if rows % 32 == 0 else 1
    remote = pl.BlockSpec(memory_space=pltpu.HBM)
    return pl.pallas_call(
        functools.partial(sweep, lats, lons),
        out_shape=jax.ShapeDtypeStruct(
            (layers, residual.shape[0], residual.shape[1], probes), jnp.float32
        ),
        in_specs=[remote, remote, remote],
        out_specs=pl.BlockSpec(memory_space=pltpu.VMEM),
        scratch_shapes=[
            pltpu.VMEM(residual.shape, jnp.bfloat16),
            pltpu.VMEM(noise_weights.shape[::-1], jnp.float32),
            pltpu.VMEM((offsets, layers, rows, cells), jnp.bfloat16),
            pltpu.VMEM((offsets + 1, chunks, rows // chunks, probes), jnp.bfloat16),
            pltpu.VMEM((layers, cells, probes), jnp.float32),
            pltpu.VMEM((lats - 1, layers, band, probes), jnp.bfloat16),
            pltpu.VMEM((lats - 1, layers, band, probes), jnp.bfloat16),
            pltpu.SemaphoreType.DMA((2,)),
            pltpu.SemaphoreType.DMA((offsets,)),
            pltpu.SemaphoreType.DMA((2 * offsets, chunks)),
            pltpu.SemaphoreType.DMA((offsets + 1, chunks)),
            pltpu.SemaphoreType.DMA((lats - 1,)),
            pltpu.SemaphoreType.DMA((lats - 1,)),
        ],
        compiler_params=pltpu.CompilerParams(
            collective_id=0, has_side_effects=True, vmem_limit_bytes=63 * 1024 * 1024
        ),
        cost_estimate=pl.CostEstimate(
            flops=2 * offsets * layers * rows * cells * probes,
            bytes_accessed=2 * offsets * layers * rows * cells,
            transcendentals=0,
        ),
    )(residual, noise_weights.T, kernel)


def solution(mesh):
    return jax.shard_map(
        functools.partial(per_device, mesh.shape["lat"], mesh.shape["lon"]),
        mesh=mesh,
        in_specs=(P("lat", "lon", None), P("lat", "lon"), P(None, None, "lat", None)),
        out_specs=P(None, "lat", "lon", None),
        check_vma=False,
    )
```

```python
import functools

import jax
import jax.numpy as jnp
from jax import lax
from jax.experimental import pallas as pl
from jax.experimental.pallas import tpu as pltpu
from jax.sharding import PartitionSpec as P

MESH = pl.DeviceIdType.MESH


def route(offsets, lons, chunks):
    direct = {d: (-d, 0) for d in range(1, offsets)}
    if lons % 2 or offsets < 3 or lons <= offsets:
        return 1, [[direct] * chunks], list(range(1, offsets))
    transit = offsets
    even, odd = [], []
    for c in range(chunks):
        if c % 2:
            even.append({**direct, 1: (-2, transit), 3: (-4, transit), transit: (1, 0)})
            odd.append({**direct, 3: (-2, 1)})
        else:
            even.append({**direct, 1: (1, 2), 3: (1, transit)})
            odd.append({**direct, 3: (-1, 2), transit: (-4, 0)})
        if offsets == 3:
            for table in (even[c], odd[c]):
                if c % 2 == 0 or table is odd[c]:
                    table.pop(transit, None)
    return 2, [even, odd], [2] + [d for d in range(offsets - 1, 0, -1) if d != 2]


def sweep(
    lats, lons, res_hbm, nw_hbm, panel_hbm, out_ref,
    res, nw, panel, blocks, total, outgoing, incoming,
    input_sem, panel_sem, east_send, east_recv, band_send, band_recv,
):
    offsets, layers, rows, cells = panel_hbm.shape
    probes = res_hbm.shape[-1]
    chunks, part = blocks.shape[1], blocks.shape[2]
    band = cells // lats
    lat, lon = lax.axis_index("lat"), lax.axis_index("lon")
    period, source, order = route(offsets, lons, chunks)
    pair = 2 if lats % 2 == 0 else 1
    groups = lats // pair

    res_load = pltpu.make_async_copy(res_hbm, res, input_sem.at[0])
    nw_load = pltpu.make_async_copy(nw_hbm, nw, input_sem.at[1])
    res_load.start()
    nw_load.start()
    loads = {}
    for d in [0] + order:
        loads[d] = pltpu.make_async_copy(panel_hbm.at[d], panel.at[d], panel_sem.at[d])
    loads[0].start()

    def along(delta):
        return (lat, lax.rem(lon + (delta + lons), lons))

    def across(a, b):
        to = lax.rem(lat // pair + a, groups) * pair + lax.rem(lat % pair + b, pair)
        return (to, lon)

    partners = [(a, b) for a in range(groups - 1, -1, -1) for b in range(pair)][: lats]
    partners = [ab for ab in partners if ab != (0, 0)]

    sends = [[[] for _ in range(chunks)] for _ in range(period)]
    senders = [set() for _ in range(period)]
    passed = [set() for _ in range(period)]
    for q in range(period):
        for c in range(chunks):
            for d, (delta, held) in sorted(source[q][c].items()):
                by = (q + delta) % period
                sends[by][c].append((-delta, held, d))
                senders[q].add(delta)
                if held > 0:
                    passed[by].add((held, c))

    def urgency(q, c, send):
        delta, _, d = send
        return ((d, c) not in passed[(q + delta) % period], c)

    receivers = [{send[0] for c in range(chunks) for send in sends[q][c]} for q in range(period)]

    def per_parity(action):
        for q in range(period):
            if period == 1:
                action(q)
            else:
                pl.when(lax.rem(lon, period) == q)(functools.partial(action, q))

    barrier = pltpu.get_barrier_semaphore()

    def greet(q):
        for delta in sorted(senders[q]):
            pl.semaphore_signal(barrier, inc=1, device_id=along(delta), device_id_type=MESH)

    per_parity(greet)
    for a, b in partners:
        pl.semaphore_signal(barrier, inc=1, device_id=across(a, b), device_id_type=MESH)

    res_load.wait()
    nw_load.wait()
    columns = res.shape[1]
    pieces = [
        nw[:, y : y + 1] * res[y].astype(jnp.float32) for y in range(rows // columns)
    ]
    weighted = jnp.concatenate(pieces, axis=0).astype(jnp.bfloat16)
    blocks[0] = weighted.reshape(chunks, part, probes)

    def east(q, n, c):
        delta, held, d = sends[q][c][n]
        return pltpu.make_async_remote_copy(
            src_ref=blocks.at[held, c],
            dst_ref=blocks.at[d, c],
            send_sem=east_send.at[n, c],
            recv_sem=east_recv.at[d, c],
            device_id=along(delta),
            device_id_type=MESH,
        )

    def begin(q):
        first = [
            (urgency(q, c, send), n, c)
            for c in range(chunks)
            for n, send in enumerate(sends[q][c])
            if send[1] == 0
        ]
        for _, n, c in sorted(first):
            east(q, n, c).start()

    def arrive(d, c):
        pltpu.make_async_remote_copy(
            src_ref=blocks.at[d, c],
            dst_ref=blocks.at[d, c],
            send_sem=east_send.at[0, c],
            recv_sem=east_recv.at[d, c],
            device_id=along(1),
            device_id_type=MESH,
        ).wait_recv()

    def admit(q):
        pl.semaphore_wait(barrier, len(receivers[q]) + len(partners))

    per_parity(admit)
    per_parity(begin)
    loads[order[0]].start()

    def product(d, l, cols):
        return lax.dot_general(
            panel[d, l, :, cols], blocks[d].reshape(rows, probes),
            (((0,), (0,)), ((), ())), preferred_element_type=jnp.float32,
        )

    def accumulate(d, first):
        loads[d].wait()
        for l in range(layers):
            for b in range(lats):
                cols = pl.ds(b * band, band)
                value = product(d, l, cols)
                total[l, cols] = value if first else total[l, cols] + value

    accumulate(0, True)
    def relay(q):
        for held, c in sorted(passed[q], key=lambda slot: (slot[0] != 2, slot[0])):
            arrive(held, c)
            for n, send in enumerate(sends[q][c]):
                if send[1] == held:
                    east(q, n, c).start()

    def rest(d, c):
        def action(q):
            if (d, c) not in passed[q]:
                arrive(d, c)

        if all((d, c) not in passed[q] for q in range(period)):
            arrive(d, c)
        else:
            per_parity(action)

    per_parity(relay)
    for d in order[1:]:
        loads[d].start()
    for d in order[:-1]:
        for c in range(chunks):
            rest(d, c)
        accumulate(d, False)

    last = order[-1]
    loads[last].wait()

    for c in range(chunks):
        rest(last, c)

    def finish(to):
        cols = pl.ds(pl.multiple_of(to * band, band), band)
        return [total[l, cols] + product(last, l, cols) for l in range(layers)]

    sent = []
    for n, (a, b) in enumerate(partners):
        to = across(a, b)
        for l, value in enumerate(finish(to[0])):
            outgoing[n, l] = value.astype(jnp.bfloat16)
        copy = pltpu.make_async_remote_copy(
            src_ref=outgoing.at[n],
            dst_ref=incoming.at[n],
            send_sem=band_send.at[n],
            recv_sem=band_recv.at[n],
            device_id=to,
            device_id_type=MESH,
        )
        copy.start()
        sent.append(copy)
    mine = finish(lat)
    for n, copy in reversed(list(enumerate(sent))):
        copy.wait_recv()
        mine = [value + incoming[n, l].astype(jnp.float32) for l, value in enumerate(mine)]
    for l, value in enumerate(mine):
        out_ref[l] = value.reshape(out_ref.shape[1:])

    def drain(q):
        for c in range(chunks):
            for n in range(len(sends[q][c])):
                east(q, n, c).wait_send()

    per_parity(drain)
    for copy in sent:
        copy.wait_send()


def per_device(lats, lons, residual, noise_weights, kernel):
    offsets, layers, rows, cells = kernel.shape
    probes = residual.shape[2]
    band = cells // lats
    chunks = 2 if rows % 32 == 0 else 1
    remote = pl.BlockSpec(memory_space=pltpu.HBM)
    return pl.pallas_call(
        functools.partial(sweep, lats, lons),
        out_shape=jax.ShapeDtypeStruct(
            (layers, residual.shape[0], residual.shape[1], probes), jnp.float32
        ),
        in_specs=[remote, remote, remote],
        out_specs=pl.BlockSpec(memory_space=pltpu.VMEM),
        scratch_shapes=[
            pltpu.VMEM(residual.shape, jnp.bfloat16),
            pltpu.VMEM(noise_weights.shape[::-1], jnp.float32),
            pltpu.VMEM((offsets, layers, rows, cells), jnp.bfloat16),
            pltpu.VMEM((offsets + 1, chunks, rows // chunks, probes), jnp.bfloat16),
            pltpu.VMEM((layers, cells, probes), jnp.float32),
            pltpu.VMEM((lats - 1, layers, band, probes), jnp.bfloat16),
            pltpu.VMEM((lats - 1, layers, band, probes), jnp.bfloat16),
            pltpu.SemaphoreType.DMA((2,)),
            pltpu.SemaphoreType.DMA((offsets,)),
            pltpu.SemaphoreType.DMA((2 * offsets, chunks)),
            pltpu.SemaphoreType.DMA((offsets + 1, chunks)),
            pltpu.SemaphoreType.DMA((lats - 1,)),
            pltpu.SemaphoreType.DMA((lats - 1,)),
        ],
        compiler_params=pltpu.CompilerParams(
            collective_id=0, has_side_effects=True, vmem_limit_bytes=63 * 1024 * 1024
        ),
        cost_estimate=pl.CostEstimate(
            flops=2 * offsets * layers * rows * cells * probes,
            bytes_accessed=2 * offsets * layers * rows * cells,
            transcendentals=0,
        ),
    )(residual, noise_weights.T, kernel)


def solution(mesh):
    return jax.shard_map(
        functools.partial(per_device, mesh.shape["lat"], mesh.shape["lon"]),
        mesh=mesh,
        in_specs=(P("lat", "lon", None), P("lat", "lon"), P(None, None, "lat", None)),
        out_specs=P(None, "lat", "lon", None),
        check_vma=False,
    )
```
